32 devices in a mesh: section: 4 (over y, x), dp: 8 (over z, core).
Axes of the slice: x: 2, y: 2, z: 4, core: 2. Of those that a mesh axis runs over, the one named last changes fastest.
Arguments:
- inputs: bfloat16 [2, 1024, 768], P(None, 'dp', 'section'), may hold values from -6 to 6
- cotangent: bfloat16 [2, 1024, 768], P(None, 'dp', 'section'), may hold values from -6 to 6
- seq_lengths: int32 [2], replicated, may hold values from 256 to 1024, as said below
- decay_rates: float32 [4, 768], P('section'), may hold values from 0.5 to 12
- norm_gain: float32 [4, 768], P('section'), may hold values from 0.5 to 1.5
- norm_bias: float32 [4, 768], P('section'), may hold values from -1.25 to 1.25
- in_weight: bfloat16 [4, 768, 2304], P('section'), may hold values from -0.21875 to 0.21875
- in_bias: float32 [4, 2304], P('section'), may hold values from -1.75 to 1.75
- short_weight: float32 [4, 3, 2304], P('section'), may hold values from -3.5 to 3.5
- short_bias: float32 [4, 2304], P('section'), may hold values from -1.75 to 1.75
- filter_weight_one: float32 [4, 33, 64], P('section'), may hold values from -1 to 1
- filter_bias_one: float32 [4, 64], P('section'), may hold values from -6 to 6
- filter_weight_two: float32 [4, 64, 64], P('section'), may hold values from -0.75 to 0.75
- filter_bias_two: float32 [4, 64], P('section'), may hold values from -6 to 6
- filter_weight_out: float32 [4, 64, 768], P('section'), may hold values from -0.0234375 to 0.0234375
- filter_bias_out: float32 [4, 768], P('section'), may hold values from -0.1875 to 0.1875
- skip_gain: float32 [4, 768], P('section'), may hold values from -6 to 6
- out_weight: bfloat16 [4, 768, 768], P('section'), may hold values from -0.21875 to 0.21875
- out_bias: float32 [4, 768], P('section'), may hold values from -1.75 to 1.75
- second_norm_gain: float32 [4, 768], P('section'), may hold values from 0.5 to 1.5
- second_norm_bias: float32 [4, 768], P('section'), may hold values from -1.25 to 1.25
- up_weight: bfloat16 [4, 768, 3072], P('section'), may hold values from -0.21875 to 0.21875
- up_bias: float32 [4, 3072], P('section'), may hold values from -1.75 to 1.75
- down_weight: bfloat16 [4, 3072, 768], P('section'), may hold values from -0.109375 to 0.109375
- down_bias: float32 [4, 768], P('section'), may hold values from -1.75 to 1.75
Outputs:
- outputs: bfloat16 [2, 1024, 768], P(None, 'dp', 'section')
- input_grad: float32 [2, 1024, 768], P(None, 'dp', 'section')
- norm_gain_grad: float32 [4, 768], P('section', 'dp')
- norm_bias_grad: float32 [4, 768], P('section', 'dp')
- in_weight_grad: float32 [4, 768, 2304], P('section', 'dp')
- in_bias_grad: float32 [4, 2304], P('section', 'dp')
- short_weight_grad: float32 [4, 3, 2304], P('section', None, 'dp')
- short_bias_grad: float32 [4, 2304], P('section', 'dp')
- filter_weight_one_grad: float32 [4, 33, 64], P('section', None, 'dp')
- filter_bias_one_grad: float32 [4, 64], P('section', 'dp')
- filter_weight_two_grad: float32 [4, 64, 64], P('section', 'dp')
- filter_bias_two_grad: float32 [4, 64], P('section', 'dp')
- filter_weight_out_grad: float32 [4, 64, 768], P('section', 'dp')
- filter_bias_out_grad: float32 [4, 768], P('section', 'dp')
- skip_gain_grad: float32 [4, 768], P('section', 'dp')
- out_weight_grad: float32 [4, 768, 768], P('section', 'dp')
- out_bias_grad: float32 [4, 768], P('section', 'dp')
- second_norm_gain_grad: float32 [4, 768], P('section', 'dp')
- second_norm_bias_grad: float32 [4, 768], P('section', 'dp')
- up_weight_grad: float32 [4, 768, 3072], P('section', 'dp')
- up_bias_grad: float32 [4, 3072], P('section', 'dp')
- down_weight_grad: float32 [4, 3072, 768], P('section', 'dp')
- down_bias_grad: float32 [4, 768], P('section', 'dp')
The draws below stay inside these ranges and needn't reach their ends.
Inputs may be any that keep to these rules, and one draw needn't show every extreme that they name: micro-batch m has seq_lengths[m] live positions at its start and padding after them; one micro-batch, drawn from the seed, has all 1024.
All inputs are finite; a program needn't handle non-finite values.
Results may differ from the reference program's by a relative error of at most 0.039.
Values may be sent and summed in bfloat16 or wider, within the bound.
A program may use at most 256 MiB of HBM per device.

```python
import math
import jax
import jax.numpy as jnp
from jax import lax

D = 768
FF = 3072
EMB = 33
FILT = 64
MICRO = 2
LAYERS = 4
TOKENS = 1024


def draw_seq_lengths(key, part):
    key = jax.random.fold_in(key, 11)
    first_key, second_key = jax.random.split(key)
    drawn = jax.random.randint(first_key, (MICRO,), TOKENS // 4, TOKENS + 1)
    chosen = jax.random.randint(second_key, (), 0, MICRO)
    return jnp.where(jnp.arange(MICRO) == chosen, TOKENS, drawn).astype(jnp.int32)


def block_levels(key, dims, shards, smallest, high):
    factor_of, own = 1.0, jax.random.fold_in(key, 6)
    for position, blocks in shards:
        steps = jnp.exp(jax.random.uniform(jax.random.fold_in(own, position), (blocks,), jnp.float32, smallest / len(shards), high / len(shards)))
        factor_of = factor_of * jnp.repeat(steps, dims[position] // blocks).reshape([-1 if axis == position else 1 for axis in range(len(dims))])
    return factor_of


def bell_draw(key, shape, scale, bound, cuts=(), dtype=jnp.bfloat16):
    entries = jax.random.normal(key, shape, jnp.float32) * scale
    if len(cuts) > 0:
        entries = block_levels(key, shape, cuts, -0.22, 0.18) * entries
    return jnp.clip(entries, min=-bound, max=bound).astype(dtype)


def setup_inputs(seed: int = 0) -> dict:
    keys = jax.random.split(jax.random.key(seed), 26)
    return {
        "inputs": bell_draw(keys[0], (MICRO, TOKENS, D), 1.0, 6.0, ((1, 8), (2, 4))),
        "cotangent": bell_draw(keys[1], (MICRO, TOKENS, D), 1.0, 6.0, ((1, 8), (2, 4))),
        "seq_lengths": draw_seq_lengths(jax.random.fold_in(keys[25], 71), 0),
        "decay_rates": jnp.clip(jnp.exp(math.log(12.0) - 3.1780538 * jax.random.uniform(keys[3], (LAYERS, D), jnp.float32) ** block_levels(keys[3], (LAYERS, D), ((0, 4),), -0.2, 0.2)), 0.5, 12.0),
        "norm_gain": jnp.clip(1.0 + 0.1 * jax.random.normal(keys[4], (LAYERS, D), jnp.float32), 0.5, 1.5),
        "norm_bias": bell_draw(keys[5], (LAYERS, D), 0.2, 1.25, ((0, 4),), jnp.float32),
        "in_weight": bell_draw(keys[6], (LAYERS, D, 3 * D), D ** -0.5, 0.21875, ((0, 4),)),
        "in_bias": bell_draw(keys[7], (LAYERS, 3 * D), 0.3, 1.75, ((0, 4),), jnp.float32),
        "short_weight": bell_draw(keys[8], (LAYERS, 3, 3 * D), 0.6, 3.5, ((0, 4),), jnp.float32),
        "short_bias": bell_draw(keys[9], (LAYERS, 3 * D), 0.3, 1.75, ((0, 4),), jnp.float32),
        "filter_weight_one": bell_draw(keys[10], (LAYERS, EMB, FILT), EMB ** -0.5, 1.0, ((0, 4),), jnp.float32),
        "filter_bias_one": bell_draw(keys[11], (LAYERS, FILT), 1.0, 6.0, ((0, 4),), jnp.float32),
        "filter_weight_two": bell_draw(keys[12], (LAYERS, FILT, FILT), FILT ** -0.5, 0.75, ((0, 4),), jnp.float32),
        "filter_bias_two": bell_draw(keys[13], (LAYERS, FILT), 1.0, 6.0, ((0, 4),), jnp.float32),
        "filter_weight_out": bell_draw(keys[14], (LAYERS, FILT, D), (FILT * TOKENS) ** -0.5, 0.0234375, ((0, 4),), jnp.float32),
        "filter_bias_out": bell_draw(keys[15], (LAYERS, D), TOKENS ** -0.5, 0.1875, ((0, 4),), jnp.float32),
        "skip_gain": bell_draw(keys[16], (LAYERS, D), 1.0, 6.0, ((0, 4),), jnp.float32),
        "out_weight": bell_draw(keys[17], (LAYERS, D, D), D ** -0.5, 0.21875, ((0, 4),)),
        "out_bias": bell_draw(keys[18], (LAYERS, D), 0.3, 1.75, ((0, 4),), jnp.float32),
        "second_norm_gain": jnp.clip(1.0 + 0.1 * jax.random.normal(keys[19], (LAYERS, D), jnp.float32), 0.5, 1.5),
        "second_norm_bias": bell_draw(keys[20], (LAYERS, D), 0.2, 1.25, ((0, 4),), jnp.float32),
        "up_weight": bell_draw(keys[21], (LAYERS, D, FF), D ** -0.5, 0.21875, ((0, 4),)),
        "up_bias": bell_draw(keys[22], (LAYERS, FF), 0.3, 1.75, ((0, 4),), jnp.float32),
        "down_weight": bell_draw(keys[23], (LAYERS, FF, D), FF ** -0.5, 0.109375, ((0, 4),)),
        "down_bias": bell_draw(keys[24], (LAYERS, D), 0.3, 1.75, ((0, 4),), jnp.float32),
    }


@jax.custom_vjp
def low(v):
    return lax.optimization_barrier(v.astype(jnp.bfloat16)).astype(jnp.float32)

@jax.custom_vjp
def low_back(v):
    return v

def low_keep(v):
    return (low(v), None)

def low_pass(kept, grad):
    return (grad,)

def back_keep(v):
    return (v, None)

def back_low(kept, grad):
    return (low(grad),)
low.defvjp(low_keep, low_pass)
low_back.defvjp(back_keep, back_low)
norm_epsilon = 1e-05
sine_scale = 14.0

def product(former, latter):
    return jnp.dot(former, latter, precision=lax.Precision.HIGHEST, preferred_element_type=jnp.float32)

def layer_norm(signal, factor, offset):
    centred = signal - lax.optimization_barrier(jnp.mean(signal, axis=-1, keepdims=True))
    spread = lax.optimization_barrier(jnp.mean(centred * centred, axis=-1, keepdims=True))
    return centred * lax.rsqrt(spread + norm_epsilon) * factor + offset

def position_features(positions, length_total):
    whole_positions = positions.astype(jnp.int32)
    scaled = whole_positions.astype(jnp.float32) / length_total
    frequency = jnp.arange(1, (EMB - 1) // 2 + 1).astype(jnp.int32)
    turn_counts = whole_positions[:, None] * frequency[None, :] % length_total
    angles = 2.0 * jnp.pi * turn_counts.astype(jnp.float32) / length_total
    return (jnp.concatenate([scaled[:, None], jnp.cos(angles), jnp.sin(angles)], axis=1), scaled)

def filter_values(first_weight, first_bias, second_weight, second_bias, third_weight, third_bias, decay_rate, features, scaled):
    layer_one = jnp.sin(sine_scale * (product(features, first_weight) + first_bias))
    layer_two = jnp.sin(sine_scale * (product(layer_one, second_weight) + second_bias))
    raw_kernel = product(layer_two, third_weight) + third_bias
    return raw_kernel * jnp.exp(-decay_rate[None, :] * scaled[:, None])

def long_conv(signal, kernel):
    length = signal.shape[0]
    spectrum = jnp.fft.rfft(signal, n=2 * length, axis=0) * jnp.fft.rfft(kernel, n=2 * length, axis=0)
    return jnp.fft.irfft(spectrum, n=2 * length, axis=0)[:length]

def block(params, decay_rate, features, scaled, carried):
    norm_gain, norm_bias, in_weight, in_bias, short_weight, short_bias, filter_weight_one, filter_bias_one, filter_weight_two, filter_bias_two, filter_weight_out, filter_bias_out, skip_gain, out_weight, out_bias, second_norm_gain, second_norm_bias, up_weight, up_bias, down_weight, down_bias = params
    normed = low(layer_norm(carried, norm_gain, norm_bias))
    mixed_rows = low_back(product(normed, in_weight) + in_bias)
    padded = jnp.concatenate([jnp.zeros((2, mixed_rows.shape[1]), jnp.float32), mixed_rows], axis=0)
    short_out = short_weight[0] * mixed_rows + short_weight[1] * padded[1:-1] + short_weight[2] * padded[:-2] + short_bias
    gate_out = short_out[:, :D]
    gate_in = short_out[:, D:2 * D]
    value = short_out[:, 2 * D:]
    kernel = filter_values(filter_weight_one, filter_bias_one, filter_weight_two, filter_bias_two, filter_weight_out, filter_bias_out, decay_rate, features, scaled)
    middle = gate_in * value
    conv_out = long_conv(middle, kernel) + skip_gain * middle
    gated_out = low(gate_out * conv_out)
    residual = carried + low_back(product(gated_out, out_weight) + out_bias)
    normed_two = low(layer_norm(residual, second_norm_gain, second_norm_bias))
    hidden = low_back(product(normed_two, up_weight) + up_bias)
    active = low(jax.nn.gelu(hidden))
    output = low_back(product(active, down_weight) + down_bias)
    return low_back(low(residual + output))

def reference(inputs, cotangent, seq_lengths, decay_rates, norm_gain, norm_bias, in_weight, in_bias, short_weight, short_bias, filter_weight_one, filter_bias_one, filter_weight_two, filter_bias_two, filter_weight_out, filter_bias_out, skip_gain, out_weight, out_bias, second_norm_gain, second_norm_bias, up_weight, up_bias, down_weight, down_bias):
    weights = tuple((tensor.astype(jnp.float32) for tensor in (norm_gain, norm_bias, in_weight, in_bias, short_weight, short_bias, filter_weight_one, filter_bias_one, filter_weight_two, filter_bias_two, filter_weight_out, filter_bias_out, skip_gain, out_weight, out_bias, second_norm_gain, second_norm_bias, up_weight, up_bias, down_weight, down_bias)))
    positions = jnp.arange(TOKENS).astype(jnp.int32)
    features, scaled = position_features(positions, TOKENS)
    checked_block = jax.checkpoint(block)

    def network(params, carried):
        for layer in range(LAYERS):
            carried = checked_block(tuple((tensor[layer] for tensor in params)), decay_rates[layer], features, scaled, carried)
        return carried

    def one_micro(running, micro_items):
        tokens, micro_grad, length = micro_items
        live_rows = (positions < length.astype(jnp.int32)).astype(jnp.float32)[:, None]

        def masked(params, carried):
            return network(params, carried) * live_rows
        result, pullback = jax.vjp(masked, weights, tokens.astype(jnp.float32))
        param_grads, entry_grad = pullback(micro_grad.astype(jnp.float32))
        updated = tuple((former + latter for former, latter in zip(running, param_grads)))
        return (updated, (result.astype(jnp.bfloat16), entry_grad))
    start = tuple((jnp.zeros_like(tensor) for tensor in weights))
    totals, (outputs, input_grad) = lax.scan(one_micro, start, (inputs, cotangent, seq_lengths))
    return (outputs, input_grad, totals[0], totals[1], totals[2], totals[3], totals[4], totals[5], totals[6], totals[7], totals[8], totals[9], totals[10], totals[11], totals[12], totals[13], totals[14], totals[15], totals[16], totals[17], totals[18], totals[19], totals[20])
```

```python
import functools
import types

import jax
import jax.numpy as jnp
import numpy as np
from jax import lax
from jax.experimental import pallas as pl
from jax.experimental.pallas import tpu as pltpu
from jax.sharding import PartitionSpec as P

MESH = pl.DeviceIdType.MESH
LANES = 128
HALO = 16
FEATURE_ROWS = 48
SMALL = 96
FAR = 6
EMB = 33


norm_epsilon = 1e-05
sine_scale = 14.0
highest = lax.Precision.HIGHEST


def as_sent(value):
    return jax.tree.map(lambda a: a.astype(jnp.bfloat16) if a.dtype == jnp.float32 else a, value)


def from_behind(value, axis, by):
    count = lax.axis_size(axis)
    pairs = [(i, i + by) for i in range(count) if 0 <= i + by < count]
    return lax.ppermute(value, axis, pairs)


def layer_norm(signal, factor, offset):
    centred = signal - jnp.mean(signal, axis=-1, keepdims=True)
    spread = jnp.mean(centred * centred, axis=-1, keepdims=True)
    return centred * lax.rsqrt(spread + norm_epsilon) * factor + offset


def exact_product(former, latter):
    return jnp.dot(former, latter, precision=highest, preferred_element_type=jnp.float32)


def low_product(former, latter):
    return jnp.dot(former, latter, preferred_element_type=jnp.float32)


def rows_product(former, latter):
    return lax.dot_general(
        former, latter, (((0,), (0,)), ((), ())), preferred_element_type=jnp.float32
    )


def back_product(former, latter):
    return lax.dot_general(
        former, latter, (((1,), (1,)), ((), ())), preferred_element_type=jnp.float32
    )


def exact_einsum(pattern, former, latter):
    return jnp.einsum(pattern, former, latter, precision=highest)


def turn_table(numerator, period):
    angles = 2.0 * jnp.pi * numerator.astype(jnp.float32) / period
    return (jnp.cos(angles), jnp.sin(angles))


def position_features(positions, length_total):
    scaled = positions.astype(jnp.float32) / length_total
    frequency = jnp.arange(1, (EMB - 1) // 2 + 1)
    turn_counts = positions[:, None] * frequency[None, :] % length_total
    angles = 2.0 * jnp.pi * turn_counts.astype(jnp.float32) / length_total
    return (jnp.concatenate([scaled[:, None], jnp.cos(angles), jnp.sin(angles)], axis=1), scaled)


def filter_values(
    first_weight,
    first_bias,
    second_weight,
    second_bias,
    third_weight,
    third_bias,
    decay_rate,
    features,
    scaled,
):
    layer_one = jnp.sin(sine_scale * (exact_product(features, first_weight) + first_bias))
    layer_two = jnp.sin(sine_scale * (exact_product(layer_one, second_weight) + second_bias))
    raw_kernel = exact_product(layer_two, third_weight) + third_bias
    return raw_kernel * jnp.exp(-decay_rate[None, :] * scaled[:, None])


def forward_transform(signal):
    part_count = lax.axis_size("dp")
    dp_index = lax.axis_index("dp")
    row_count = signal.shape[0]
    block_rows = row_count // part_count
    transform_size = 2 * part_count * row_count
    spread_rows = lax.all_to_all(
        signal.reshape(part_count, block_rows, -1).astype(jnp.bfloat16),
        "dp",
        split_axis=0,
        concat_axis=0,
        tiled=True,
    ).astype(jnp.float32)
    coarse = jnp.arange(2 * part_count)
    coarse_cos, coarse_sin = turn_table(
        coarse[:, None] * jnp.arange(part_count)[None, :] % (2 * part_count), 2 * part_count
    )
    real_first = exact_einsum("kp,pmc->kmc", coarse_cos, spread_rows)
    imag_first = -exact_einsum("kp,pmc->kmc", coarse_sin, spread_rows)
    offsets = dp_index * block_rows + jnp.arange(block_rows)
    twist_cos, twist_sin = turn_table(
        coarse[:, None] * offsets[None, :] % transform_size, transform_size
    )
    twist_cos = twist_cos[:, :, None]
    twist_sin = twist_sin[:, :, None]
    real_twist = real_first * twist_cos + imag_first * twist_sin
    imag_twist = imag_first * twist_cos - real_first * twist_sin
    real_group, imag_group = (
        lax.all_to_all(as_sent(real_twist), "dp", split_axis=0, concat_axis=1, tiled=True).astype(
            real_twist.dtype
        ),
        lax.all_to_all(as_sent(imag_twist), "dp", split_axis=0, concat_axis=1, tiled=True).astype(
            imag_twist.dtype
        ),
    )
    fine_index = jnp.arange(row_count)
    fine_cos, fine_sin = turn_table(
        fine_index[:, None] * fine_index[None, :] % row_count, row_count
    )
    real_out = exact_einsum("km,jmc->jkc", fine_cos, real_group) + exact_einsum(
        "km,jmc->jkc", fine_sin, imag_group
    )
    imag_out = exact_einsum("km,jmc->jkc", fine_cos, imag_group) - exact_einsum(
        "km,jmc->jkc", fine_sin, real_group
    )
    return (real_out, imag_out)


def inverse_transform(real_part, imag_part):
    part_count = lax.axis_size("dp")
    dp_index = lax.axis_index("dp")
    row_count = real_part.shape[1]
    transform_size = 2 * part_count * row_count
    fine_index = jnp.arange(row_count)
    fine_cos, fine_sin = turn_table(
        fine_index[:, None] * fine_index[None, :] % row_count, row_count
    )
    real_first = exact_einsum("mk,jkc->jmc", fine_cos, real_part) - exact_einsum(
        "mk,jkc->jmc", fine_sin, imag_part
    )
    imag_first = exact_einsum("mk,jkc->jmc", fine_cos, imag_part) + exact_einsum(
        "mk,jkc->jmc", fine_sin, real_part
    )
    coarse_local = 2 * dp_index + jnp.arange(2)
    twist_cos, twist_sin = turn_table(
        coarse_local[:, None] * fine_index[None, :] % transform_size, transform_size
    )
    twist_cos = twist_cos[:, :, None]
    twist_sin = twist_sin[:, :, None]
    real_twist = real_first * twist_cos - imag_first * twist_sin
    imag_twist = imag_first * twist_cos + real_first * twist_sin
    real_group, imag_group = (
        lax.all_to_all(as_sent(real_twist), "dp", split_axis=1, concat_axis=0, tiled=True).astype(
            real_twist.dtype
        ),
        lax.all_to_all(as_sent(imag_twist), "dp", split_axis=1, concat_axis=0, tiled=True).astype(
            imag_twist.dtype
        ),
    )
    coarse = jnp.arange(2 * part_count)
    coarse_cos, coarse_sin = turn_table(
        jnp.arange(part_count)[:, None] * coarse[None, :] % (2 * part_count), 2 * part_count
    )
    values = (
        exact_einsum("pk,kmc->pmc", coarse_cos, real_group)
        - exact_einsum("pk,kmc->pmc", coarse_sin, imag_group)
    ) / transform_size
    returned = lax.all_to_all(
        as_sent(values), "dp", split_axis=0, concat_axis=1, tiled=True
    ).astype(values.dtype)
    return returned.reshape(row_count, -1)


def spectral_product(former, latter, conjugate):
    former_real, former_imag = former
    latter_real, latter_imag = latter
    if conjugate:
        former_imag = -former_imag
    return (
        former_real * latter_real - former_imag * latter_imag,
        former_real * latter_imag + former_imag * latter_real,
    )


def block_forward(weights, spectrum, hidden_state):
    (
        norm_gain,
        norm_bias,
        in_weight,
        in_bias,
        short_weight,
        short_bias,
        filter_weight_one,
        filter_bias_one,
        filter_weight_two,
        filter_bias_two,
        filter_weight_out,
        filter_bias_out,
        skip_gain,
        out_weight,
        out_bias,
        second_norm_gain,
        second_norm_bias,
        up_weight,
        up_bias,
        down_weight,
        down_bias,
    ) = weights
    model_width = norm_gain.shape[0]
    normed = layer_norm(hidden_state, norm_gain, norm_bias).astype(jnp.bfloat16)
    mixed_rows = low_product(normed, in_weight) + in_bias
    before = from_behind(mixed_rows[-2:], "dp", 1)
    padded = jnp.concatenate([before, mixed_rows], axis=0)
    short_out = (
        short_weight[0] * mixed_rows
        + short_weight[1] * padded[1:-1]
        + short_weight[2] * padded[:-2]
        + short_bias
    )
    gate_out = short_out[:, :model_width]
    gate_in = short_out[:, model_width : 2 * model_width]
    value = short_out[:, 2 * model_width :]
    middle = gate_in * value
    spectrum_mid = forward_transform(middle)
    conv_out = (
        inverse_transform(*spectral_product(spectrum_mid, spectrum, False)) + skip_gain * middle
    )
    gated_out = (gate_out * conv_out).astype(jnp.bfloat16)
    residual = hidden_state + (low_product(gated_out, out_weight) + out_bias)
    normed_two = layer_norm(residual, second_norm_gain, second_norm_bias).astype(jnp.bfloat16)
    hidden = low_product(normed_two, up_weight) + up_bias
    active = jax.nn.gelu(hidden).astype(jnp.bfloat16)
    output = (residual + (low_product(active, down_weight) + down_bias)).astype(jnp.bfloat16)
    stashed = (
        hidden_state,
        normed,
        mixed_rows,
        before,
        short_out,
        middle,
        spectrum_mid,
        conv_out,
        gated_out,
        residual,
        normed_two,
        hidden,
        active,
    )
    kept = (hidden_state, before, short_out, middle, spectrum_mid, conv_out, gated_out)
    return (output, stashed, kept)


def block_backward(weights, spectrum, stashed, grad_out):
    (
        norm_gain,
        norm_bias,
        in_weight,
        in_bias,
        short_weight,
        short_bias,
        filter_weight_one,
        filter_bias_one,
        filter_weight_two,
        filter_bias_two,
        filter_weight_out,
        filter_bias_out,
        skip_gain,
        out_weight,
        out_bias,
        second_norm_gain,
        second_norm_bias,
        up_weight,
        up_bias,
        down_weight,
        down_bias,
    ) = weights
    (
        hidden_state,
        normed,
        mixed_rows,
        before,
        short_out,
        middle,
        spectrum_mid,
        conv_out,
        gated_out,
        residual,
        normed_two,
        hidden,
        active,
    ) = stashed
    model_width = norm_gain.shape[0]
    gate_out = short_out[:, :model_width]
    gate_in = short_out[:, model_width : 2 * model_width]
    value = short_out[:, 2 * model_width :]
    grad_low = grad_out.astype(jnp.bfloat16)
    down_grad = rows_product(active, grad_low)
    down_bias_grad = jnp.sum(grad_low.astype(jnp.float32), axis=0)
    grad_active = back_product(grad_low, down_weight)
    _, gelu_pullback = jax.vjp(jax.nn.gelu, hidden)
    grad_hidden = gelu_pullback(grad_active)[0].astype(jnp.bfloat16)
    up_grad = rows_product(normed_two, grad_hidden)
    up_bias_grad = jnp.sum(grad_hidden.astype(jnp.float32), axis=0)
    _, second_pullback = jax.vjp(layer_norm, residual, second_norm_gain, second_norm_bias)
    grad_norm_res, second_gain_grad, second_bias_grad = second_pullback(
        back_product(grad_hidden, up_weight)
    )
    grad_residual = grad_low.astype(jnp.float32) + grad_norm_res
    grad_branch = grad_residual.astype(jnp.bfloat16)
    out_grad = rows_product(gated_out, grad_branch)
    out_bias_grad = jnp.sum(grad_branch.astype(jnp.float32), axis=0)
    grad_gated = back_product(grad_branch, out_weight)
    grad_conv = grad_gated * gate_out
    grad_gate_out = grad_gated * conv_out
    skip_grad = jnp.sum(grad_conv * middle, axis=0)
    grad_spectrum = forward_transform(grad_conv)
    grad_middle = skip_gain * grad_conv + inverse_transform(
        *spectral_product(spectrum, grad_spectrum, True)
    )
    kernel_grad = spectral_product(spectrum_mid, grad_spectrum, True)
    grad_gate_in = grad_middle * value
    grad_value = grad_middle * gate_in
    grad_short = jnp.concatenate([grad_gate_out, grad_gate_in, grad_value], axis=1)
    after_rows = from_behind(grad_short[:2], "dp", -1)
    extended = jnp.concatenate([grad_short, after_rows], axis=0)
    padded = jnp.concatenate([before, mixed_rows], axis=0)
    short_grad = jnp.stack(
        [
            jnp.sum(grad_short * mixed_rows, axis=0),
            jnp.sum(grad_short * padded[1:-1], axis=0),
            jnp.sum(grad_short * padded[:-2], axis=0),
        ]
    )
    short_bias_grad = jnp.sum(grad_short, axis=0)
    grad_mixed = (
        short_weight[0] * grad_short
        + short_weight[1] * extended[1:-1]
        + short_weight[2] * extended[2:]
    ).astype(jnp.bfloat16)
    in_grad = rows_product(normed, grad_mixed)
    in_bias_grad = jnp.sum(grad_mixed.astype(jnp.float32), axis=0)
    _, first_pullback = jax.vjp(layer_norm, hidden_state, norm_gain, norm_bias)
    grad_norm_in, gain_grad, bias_grad = first_pullback(back_product(grad_mixed, in_weight))
    grad_state = grad_residual + grad_norm_in
    grads = (
        gain_grad,
        bias_grad,
        in_grad,
        in_bias_grad,
        short_grad,
        short_bias_grad,
        skip_grad,
        out_grad,
        out_bias_grad,
        second_gain_grad,
        second_bias_grad,
        up_grad,
        up_bias_grad,
        down_grad,
        down_bias_grad,
    )
    return (grad_state, grads, kernel_grad)


def local_general(
    inputs,
    cotangent,
    seq_lengths,
    decay_rates,
    norm_gain,
    norm_bias,
    in_weight,
    in_bias,
    short_weight,
    short_bias,
    filter_weight_one,
    filter_bias_one,
    filter_weight_two,
    filter_bias_two,
    filter_weight_out,
    filter_bias_out,
    skip_gain,
    out_weight,
    out_bias,
    second_norm_gain,
    second_norm_bias,
    up_weight,
    up_bias,
    down_weight,
    down_bias,
):
    sections = lax.axis_size("section")
    section_index = lax.axis_index("section")
    part_count = lax.axis_size("dp")
    dp_index = lax.axis_index("dp")
    whole_in, whole_grad = (
        lax.all_gather(inputs, "section", axis=2, tiled=True),
        lax.all_gather(cotangent, "section", axis=2, tiled=True),
    )
    micro_count, row_count, model_width = whole_in.shape
    weights = tuple(
        (
            tensor[0]
            for tensor in (
                norm_gain,
                norm_bias,
                in_weight,
                in_bias,
                short_weight,
                short_bias,
                filter_weight_one,
                filter_bias_one,
                filter_weight_two,
                filter_bias_two,
                filter_weight_out,
                filter_bias_out,
                skip_gain,
                out_weight,
                out_bias,
                second_norm_gain,
                second_norm_bias,
                up_weight,
                up_bias,
                down_weight,
                down_bias,
            )
        )
    )
    decay_rate = decay_rates[0]
    positions = dp_index * row_count + jnp.arange(row_count)
    features, scaled = position_features(positions, part_count * row_count)
    live_rows = (positions[None, :] < seq_lengths[:, None]).astype(jnp.float32)
    tick_count = micro_count + sections - 1
    fixed_spectrum = forward_transform(filter_values(*weights[6:12], decay_rate, features, scaled))

    def forward_tick(incoming, tick_index):
        slot_index = jnp.clip(tick_index - section_index, 0, micro_count - 1)
        hidden_state = jnp.where(section_index == 0, whole_in[slot_index], incoming).astype(
            jnp.float32
        )
        output, stashed, kept = block_forward(weights, fixed_spectrum, hidden_state)
        passed = from_behind(output, "section", 1)
        return (passed, (output, stashed))

    start_rows = jnp.zeros((row_count, model_width), jnp.bfloat16)
    _, (outputs_all, stash) = lax.scan(forward_tick, start_rows, jnp.arange(tick_count))
    chosen = (0, 1, 2, 3, 4, 5, 12, 13, 14, 15, 16, 17, 18, 19, 20)
    start_totals = tuple((jnp.zeros(weights[position].shape, jnp.float32) for position in chosen))
    kernel_zero = jnp.zeros(fixed_spectrum[0].shape, jnp.float32)

    def backward_tick(carry, tick_index):
        incoming, totals, kernel_total = carry
        micro_index = tick_index - (sections - 1 - section_index)
        is_valid = (micro_index >= 0) & (micro_index < micro_count)
        slot_index = jnp.clip(micro_index, 0, micro_count - 1)
        top_grad = whole_grad[slot_index].astype(jnp.float32) * live_rows[slot_index][:, None]
        grad_out = jnp.where(section_index == sections - 1, top_grad, incoming.astype(jnp.float32))
        stashed = jax.tree.map(lambda buffer: buffer[slot_index + section_index], stash)
        grad_state, grads, kernel_grad = block_backward(weights, fixed_spectrum, stashed, grad_out)
        totals = jax.tree.map(
            lambda running, addend: running + jnp.where(is_valid, addend, 0.0), totals, grads
        )
        kernel_total = jax.tree.map(
            lambda running, addend: running + jnp.where(is_valid, addend, 0.0),
            kernel_total,
            kernel_grad,
        )
        passed = from_behind(grad_state.astype(jnp.bfloat16), "section", -1)
        return ((passed, totals, kernel_total), grad_state)

    carry_start = (start_rows, start_totals, (kernel_zero, kernel_zero))
    (_, totals, kernel_total), grads_in = lax.scan(
        backward_tick, carry_start, jnp.arange(tick_count)
    )
    kernel_grad = inverse_transform(*kernel_total)

    def filter_local(weight_one, bias_one, weight_two, bias_two, weight_out, bias_out):
        return filter_values(
            weight_one,
            bias_one,
            weight_two,
            bias_two,
            weight_out,
            bias_out,
            decay_rate,
            features,
            scaled,
        )

    _, filter_pullback = jax.vjp(filter_local, *weights[6:12])
    filter_grads = tuple(filter_pullback(kernel_grad))
    all_grads = totals[:6] + filter_grads + totals[6:]
    summed = (
        lax.psum_scatter(all_grads[0], "dp", scatter_dimension=0, tiled=True),
        lax.psum_scatter(all_grads[1], "dp", scatter_dimension=0, tiled=True),
        lax.psum_scatter(all_grads[2], "dp", scatter_dimension=0, tiled=True),
        lax.psum_scatter(all_grads[3], "dp", scatter_dimension=0, tiled=True),
        lax.psum_scatter(all_grads[4], "dp", scatter_dimension=1, tiled=True),
        lax.psum_scatter(all_grads[5], "dp", scatter_dimension=0, tiled=True),
        lax.psum_scatter(all_grads[6], "dp", scatter_dimension=1, tiled=True),
        lax.psum_scatter(all_grads[7], "dp", scatter_dimension=0, tiled=True),
        lax.psum_scatter(all_grads[8], "dp", scatter_dimension=0, tiled=True),
        lax.psum_scatter(all_grads[9], "dp", scatter_dimension=0, tiled=True),
        lax.psum_scatter(all_grads[10], "dp", scatter_dimension=0, tiled=True),
        lax.psum_scatter(all_grads[11], "dp", scatter_dimension=0, tiled=True),
        lax.psum_scatter(all_grads[12], "dp", scatter_dimension=0, tiled=True),
        lax.psum_scatter(all_grads[13], "dp", scatter_dimension=0, tiled=True),
        lax.psum_scatter(all_grads[14], "dp", scatter_dimension=0, tiled=True),
        lax.psum_scatter(all_grads[15], "dp", scatter_dimension=0, tiled=True),
        lax.psum_scatter(all_grads[16], "dp", scatter_dimension=0, tiled=True),
        lax.psum_scatter(all_grads[17], "dp", scatter_dimension=0, tiled=True),
        lax.psum_scatter(all_grads[18], "dp", scatter_dimension=0, tiled=True),
        lax.psum_scatter(all_grads[19], "dp", scatter_dimension=0, tiled=True),
        lax.psum_scatter(all_grads[20], "dp", scatter_dimension=0, tiled=True),
    )
    final_rows = (
        outputs_all[sections - 1 : sections - 1 + micro_count].astype(jnp.float32)
        * live_rows[:, :, None]
    )
    final_rows = jnp.where(section_index == sections - 1, final_rows, 0.0)
    entry_grad = jnp.where(
        section_index == 0, grads_in[sections - 1 : sections - 1 + micro_count], 0.0
    )
    shown_rows, input_grad = (
        lax.psum_scatter(
            final_rows.astype(jnp.bfloat16), "section", scatter_dimension=2, tiled=True
        ).astype(jnp.float32),
        lax.psum_scatter(
            entry_grad.astype(jnp.bfloat16), "section", scatter_dimension=2, tiled=True
        ).astype(jnp.float32),
    )
    return (shown_rows.astype(jnp.bfloat16), input_grad) + tuple(
        (summed_grad[None] for summed_grad in summed)
    )


def dot_nn(a, b):
    return lax.dot_general(a, b, (((1,), (0,)), ((), ())), preferred_element_type=jnp.float32)


def dot_nt(a, b):
    return lax.dot_general(a, b, (((1,), (1,)), ((), ())), preferred_element_type=jnp.float32)


def col_sum(a):
    return jnp.sum(a, axis=0, keepdims=True)


def normalized(signal):
    middle = jnp.mean(signal, axis=-1, keepdims=True)
    centred = signal - middle
    spread = jnp.mean(centred * centred, axis=-1, keepdims=True)
    inverse = lax.rsqrt(spread + norm_epsilon)
    return (centred * inverse, middle, inverse)


def norm_backward(grad, unit, inverse, factor):
    scaled = grad * factor
    first = jnp.mean(scaled, axis=-1, keepdims=True)
    second = jnp.mean(scaled * unit, axis=-1, keepdims=True)
    return inverse * (scaled - first - unit * second)


GELU_ROOT = float(np.sqrt(2.0 / np.pi))
GELU_CUBE = 0.044715


def gelu_half(v, square):
    return 0.5 + 0.5 * jnp.tanh(v * (GELU_ROOT + (GELU_ROOT * GELU_CUBE) * square))


def gelu(v):
    return v * gelu_half(v, v * v)


def gelu_slope(v):
    square = v * v
    half = gelu_half(v, square)
    inner = v * (2.0 * GELU_ROOT + (6.0 * GELU_ROOT * GELU_CUBE) * square)
    return half * (1.0 + (1.0 - half) * inner)


def turned(block):
    return block.astype(jnp.float32).T.astype(jnp.bfloat16)


def aligned(value, by):
    return pl.multiple_of(value, by)


def halves(value):
    high = value.astype(jnp.bfloat16)
    return high, (value - high.astype(jnp.float32)).astype(jnp.bfloat16)


def fine_left(value):
    high, low = halves(value)
    return jnp.concatenate([high, low, high], axis=1)


def fine_right(value):
    high, low = halves(value)
    return jnp.concatenate([high, high, low], axis=0)


def filter_layers(r, part):
    first = r.filter_one[:, 0, :]
    rest = jnp.zeros((FEATURE_ROWS - first.shape[0], first.shape[1]), jnp.float32)
    first = jnp.concatenate([first, rest], axis=0)
    one = sine_scale * (dot_nn(r.features[part], fine_right(first)) + r.filter_one_bias[...])
    layer_one = jnp.sin(one)
    two = dot_nn(fine_left(layer_one), fine_right(r.filter_two[...]))
    two = sine_scale * (two + r.filter_two_bias[...])
    return (layer_one, jnp.sin(two), one, two)


def chain_kernel(geometry, names, *all_refs):
    sections, parts, group, rows, width, hidden_width = geometry
    r = types.SimpleNamespace(**dict(zip(names, all_refs)))
    total = group * rows
    blocks = width // LANES
    share = width // sections
    held = total // parts
    s = lax.axis_index("section")
    e = lax.axis_index("dp")
    q = e // group
    flipped = lax.rem(q, 2) == 1
    i = jnp.where(flipped, group - 1 - e % group, e % group)
    following = jnp.where(flipped, e - 1, e + 1)
    preceding = jnp.where(flipped, e + 1, e - 1)
    mate_core = e + 1 - 2 * lax.rem(e, 2)
    first_of_group = q * group

    def remote(src, dst, send, recv, section, dp):
        return pltpu.make_async_remote_copy(
            src_ref=src,
            dst_ref=dst,
            send_sem=send,
            recv_sem=recv,
            device_id={"section": section, "dp": dp},
            device_id_type=MESH,
        )

    def arrived(dst, recv):
        remote(dst, dst, recv, recv, s, e).wait_recv()

    def sent(src, send):
        remote(src, src, send, send, s, e).wait_send()

    def start_to(src, dst, send, recv, section, dp):
        here = (section == s) & (dp == e)

        @pl.when(here)
        def _():
            pltpu.make_async_copy(src, dst, recv).start()

        @pl.when(jnp.logical_not(here))
        def _():
            remote(src, dst, send, recv, section, dp).start()

    def sent_to(src, send, section, dp):
        here = (section == s) & (dp == e)

        @pl.when(jnp.logical_not(here))
        def _():
            sent(src, send)

    barrier = pltpu.get_barrier_semaphore()
    me = s * parts + e
    devices = sections * parts

    def greet(step, carry):
        there = lax.rem(me + step, devices)
        pl.semaphore_signal(
            barrier,
            inc=1,
            device_id={"section": there // parts, "dp": lax.rem(there, parts)},
            device_id_type=MESH,
        )
        return carry

    lax.fori_loop(1, devices, greet, 0)

    def load(there, here, index):
        copy = pltpu.make_async_copy(there, here, r.load_sem.at[index])
        copy.start()
        return copy

    load_in = load(r.w_in, r.v_in, 0)
    load_out = load(r.w_out, r.v_out, 1)
    load_up = load(r.w_up, r.v_up, 2)
    load_down = load(r.w_down, r.v_down, 3)

    pl.semaphore_wait(barrier, devices - 1)

    pos, low_half = e // 2, e % 2
    micro = r.inputs.shape[0]
    last = sections - 1
    halo_there = (low_half == 1) & (pos < group - 1)
    def holder(m, place):
        return m * group + (group - 1 - place if m % 2 else place)

    for m in range(micro):
        dp = holder(m, pos)
        start_to(
            r.inputs.at[m],
            r.in_recv.at[low_half, pl.ds(aligned(s * share, share), share)],
            r.in_send_sem.at[m],
            r.in_sem.at[s, low_half],
            0,
            dp,
        )

        @pl.when(halo_there)
        def _():
            start_to(
                r.inputs.at[m],
                r.in_halo.at[pl.ds(aligned(s * share, share), share)],
                r.halo_send_sem.at[m],
                r.halo_sem.at[s],
                0,
                holder(m, pos + 1),
            )


    def send_cotangent():
        for m in range(micro):
            start_to(
                r.cot.at[m],
                r.cot_recv.at[low_half, pl.ds(aligned(s * share, share), share)],
                r.cot_send_sem.at[m],
                r.cot_sem.at[s, low_half],
                last,
                holder(m, pos),
            )

    wide = 2 * LANES
    pieces = width // wide
    sign = 1.0 - 2.0 * lax.rem(
        lax.broadcasted_iota(jnp.int32, (rows, 1), 0), jnp.int32(2)
    ).astype(jnp.float32)

    def chunk_of(k, offset=0):
        return pl.ds(offset + k * wide, wide)

    def scaled_place(m):
        place = lax.broadcasted_iota(jnp.int32, (rows, 1), 0) + m * rows
        return place.astype(jnp.float32) * (1.0 / total)

    def filter_step(m, carry):
        part = pl.ds(aligned(m * rows, rows), rows)
        fine = fine_left(filter_layers(r, part)[1])
        for k in range(pieces):
            cols = chunk_of(k)
            raw = dot_nn(fine, fine_right(r.filter_out[:, cols])) + r.filter_out_bias[:, cols]
            value = raw * jnp.exp(-r.decay[:, cols] * scaled_place(m))
            spec = dot_nn(r.waves[...], value.astype(jnp.bfloat16))
            upper, lower = pl.ds(2 * k * wide, wide), pl.ds((2 * k + 1) * wide, wide)
            even = jnp.where(m > 0, r.gs[pl.ds(0, rows), upper], 0.0)
            odd = jnp.where(m > 0, r.gs[pl.ds(0, rows), lower], 0.0)
            r.kspec[m, k, :rows] = (spec[:rows] + sign * odd).astype(jnp.bfloat16)
            r.kspec[m, k, rows:] = (spec[rows:] - sign * even).astype(jnp.bfloat16)
            r.gs[pl.ds(0, rows), upper] = spec[:rows]
            r.gs[pl.ds(0, rows), lower] = spec[rows:]
        return carry

    @pl.when(s > 0)
    def _():
        lax.fori_loop(0, group, filter_step, 0)
        send_cotangent()

    def order(back):
        return (group - 1 - i) if back else i

    def mate(n, back):
        place = (group - 1 - n) if back else n
        return first_of_group + jnp.where(flipped, group - 1 - place, place)

    def hop(src, back, slot, k, send, there):
        lanes = r.far_back if back else r.far
        arrive = r.far_back_sem if back else r.far_sem
        return remote(src, lanes.at[slot, k], send, arrive.at[slot, k], s, mate(there, back))

    direct = ((0, 2), (0, 1), (1, 3), (2, 3))
    handed = ((2, 3, 0), (3, 2, 1))

    def send_piece(src, k, back):
        send = r.near_back_send_sem if back else r.near_send_sem
        for index, (here, there) in enumerate(direct):

            @pl.when(order(back) == here)
            def _():
                hop(src.at[k], back, here, k, send.at[index % 2, k], there).start()

    def pieces_sent(src, back):
        send = r.near_back_send_sem if back else r.near_send_sem
        for index, (here, there) in enumerate(direct):

            @pl.when(order(back) == here)
            def _():
                for k in range(pieces):
                    sent(src.at[k], send.at[index % 2, k])

        hand = r.hand_back_send_sem if back else r.hand_send_sem
        lanes = r.far_back if back else r.far
        for here, there, slot in handed:

            @pl.when(order(back) == here)
            def _():
                for k in range(pieces):
                    sent(lanes.at[slot, k], hand.at[k])

    def transform(src, into):
        value = dot_nn(r.waves[...], jnp.concatenate([src[k] for k in range(pieces)], axis=1))
        for k in range(pieces):
            into[k] = value[:, k * wide : (k + 1) * wide].astype(jnp.bfloat16)

    def far_from(slot, back):
        lanes = r.far_back if back else r.far
        arrive = r.far_back_sem if back else r.far_sem
        for k in range(pieces):
            arrived(lanes.at[slot, k], arrive.at[slot, k])

    def transform_far(slot, back):
        lanes = r.far_back if back else r.far
        specs = r.wspec if back else r.zspec
        transform(lanes.at[slot], specs.at[slot])

    def other_chip(back):
        lanes = r.far_back if back else r.far
        hand = r.hand_back_send_sem if back else r.hand_send_sem
        for here, there, slot in handed:

            @pl.when(order(back) == here)
            def _():
                arrive = r.far_back_sem if back else r.far_sem
                for k in range(pieces):
                    arrived(lanes.at[slot, k], arrive.at[slot, k])
                    hop(lanes.at[slot, k], back, slot, k, hand.at[k], there).start()
                transform_far(slot, back)
                far_from(1 - slot, back)
                transform_far(1 - slot, back)

    def other_core(back):
        for n in (1, 3):

            @pl.when(order(back) == n)
            def _():
                far_from(n - 1, back)
                transform_far(n - 1, back)

    fine_rows = 32

    def combine(back, n, sources, first, final):
        specs = r.wspec if back else r.zspec

        def rows_step(step, carry):
            k = step // (rows // fine_rows)
            start = aligned(lax.rem(step, rows // fine_rows) * fine_rows, fine_rows)
            upper, lower = pl.ds(start, fine_rows), pl.ds(rows + start, fine_rows)
            lanes = aligned(width + 2 * k * wide, wide)
            even_place = (pl.ds(start, fine_rows), pl.ds(lanes, wide))
            odd_place = (pl.ds(start, fine_rows), pl.ds(lanes + wide, wide))
            even = odd = 0.0
            if not first:
                even, odd = r.gs[even_place], r.gs[odd_place]
            for j in sources:
                a = specs[j, k, upper].astype(jnp.float32)
                b = specs[j, k, lower].astype(jnp.float32)
                u = r.kspec[n - j, k, upper].astype(jnp.float32)
                v = r.kspec[n - j, k, lower].astype(jnp.float32)
                if back:
                    even, odd = even + a * u + b * v, odd + b * u - a * v
                else:
                    even, odd = even + a * u - b * v, odd + a * v + b * u
            if final:
                r.yspec[k, upper] = even.astype(jnp.bfloat16)
                r.yspec[k, lower] = odd.astype(jnp.bfloat16)
            else:
                r.gs[even_place] = even
                r.gs[odd_place] = odd
            return carry

        lax.fori_loop(0, pieces * (rows // fine_rows), rows_step, 0)

    def combine_far(back):
        for n in (2, 3):

            @pl.when(order(back) == n)
            def _():
                combine(back, n, (0, 1), True, False)

    def combine_near(back):
        for n in range(group):

            @pl.when(order(back) == n)
            def _():
                if n < 2:
                    combine(back, n, range(n + 1), True, True)
                else:
                    combine(back, n, range(2, n + 1), False, True)

    def inverse():
        spec = jnp.concatenate([r.yspec[k] for k in range(pieces)], axis=1)
        return dot_nn(r.waves_back[...], spec) * (1.0 / rows)

    @pl.when(s > 0)
    def _():
        other_chip(False)
        combine_far(False)

    @pl.when(s == last)
    def _():
        length = r.lengths[q]
        for section in range(sections):
            for h in range(2):
                arrived(
                    r.cot_recv.at[h, pl.ds(section * share, share)], r.cot_sem.at[section, h]
                )
        for h in range(2):
            part = pl.ds(h * (rows // 2), rows // 2)
            place = lax.broadcasted_iota(jnp.int32, (rows // 2, 1), 0) + i * rows + h * (rows // 2)
            live = (place < length).astype(jnp.float32)
            r.g[part] = (turned(r.cot_recv[h]).astype(jnp.float32) * live).astype(jnp.bfloat16)

    @pl.when(s == 0)
    def _():
        for section in range(sections):
            for h in range(2):
                arrived(
                    r.in_recv.at[h, pl.ds(section * share, share)], r.in_sem.at[section, h]
                )
        for h in range(2):
            start = HALO + h * held
            r.x[start : start + held] = turned(r.in_recv[h])

        @pl.when(i > 0)
        def _():
            for section in range(sections):
                arrived(
                    r.in_halo.at[pl.ds(section * share, share)], r.halo_sem.at[section]
                )
            r.x[:HALO] = turned(r.in_halo[...])[held - HALO :]

    @pl.when(s > 0)
    def _():
        arrived(r.x.at[pl.ds(HALO, rows)], r.pass_sem.at[0])

        @pl.when(i > 0)
        def _():
            arrived(r.x.at[pl.ds(0, HALO)], r.pass_sem.at[1])

    def norm_rows(start, count):
        unit, middle, inverse = normalized(r.x[pl.ds(start, count)].astype(jnp.float32))
        r.stats[pl.ds(start, count), 0:1] = middle
        r.stats[pl.ds(start, count), 1:2] = inverse
        r.normed[pl.ds(start, count)] = (
            unit * r.norm_gain[...] + r.norm_bias[...]
        ).astype(jnp.bfloat16)

    norm_rows(0, HALO)
    chunk = 128

    def norm_step(step, carry):
        norm_rows(aligned(HALO + step * chunk, HALO), chunk)
        return carry

    lax.fori_loop(0, rows // chunk, norm_step, 0)
    load_in.wait()

    def mix(cols):
        value = dot_nn(r.normed[...], r.v_in[:, cols]) + r.in_bias[:, cols]
        r.mixed[pl.ds(HALO, rows), cols] = value[HALO:]
        r.mixed[:HALO, cols] = jnp.where(i > 0, value[:HALO], 0.0)

    for k in (1, 2):
        mix(pl.ds(k * width, width))

    def lanes_of(block, offset=0):
        return pl.ds(aligned(offset + block * LANES, LANES), LANES)

    def short_conv(cols):
        here = r.mixed[pl.ds(HALO, rows), cols]
        one = r.mixed[pl.ds(HALO - 1, rows), cols]
        two = r.mixed[pl.ds(HALO - 2, rows), cols]
        w = r.short_weight
        value = w[0, :, cols] * here + w[1, :, cols] * one + w[2, :, cols] * two
        value = value + r.short_bias[:, cols]
        r.short[:, cols] = value
        return value

    for k in range(pieces):
        gate = short_conv(chunk_of(k, width))
        value = short_conv(chunk_of(k, 2 * width))
        r.mid_send[k] = (gate * value).astype(jnp.bfloat16)
        mix(chunk_of(k))
        send_piece(r.mid_send, k, False)
    transform(r.mid_send, r.zspec.at[i])
    for k in range(pieces):
        short_conv(chunk_of(k))

    @pl.when(s == 0)
    def _():
        lax.fori_loop(0, group, filter_step, 0)
        send_cotangent()

    @pl.when(s == 0)
    def _():
        other_chip(False)
        combine_far(False)

    other_core(False)
    combine_near(False)
    found = inverse()
    for k in range(pieces):
        cols = chunk_of(k)
        middle = r.short[:, chunk_of(k, width)] * r.short[:, chunk_of(k, 2 * width)]
        conv = found[:, k * wide : (k + 1) * wide] + r.skip_gain[:, cols] * middle
        r.conv_out[:, cols] = conv
        r.gated[:, cols] = (r.short[:, cols] * conv).astype(jnp.bfloat16)
    load_out.wait()
    r.residual[...] = (
        dot_nn(r.gated[...], r.v_out[...])
        + r.out_bias[...]
        + r.x[pl.ds(HALO, rows)].astype(jnp.float32)
    )

    def norm_two_step(step, carry):
        part = pl.ds(aligned(step * chunk, chunk), chunk)
        value = r.residual[part]
        unit, middle, inverse = normalized(value)
        r.stats[part, 2:3] = middle
        r.stats[part, 3:4] = inverse
        r.normed_two[part] = (
            unit * r.second_norm_gain[...] + r.second_norm_bias[...]
        ).astype(jnp.bfloat16)
        return carry

    lax.fori_loop(0, rows // chunk, norm_two_step, 0)
    load_up.wait()
    load_down.wait()

    feed_steps = hidden_width // width
    for k in range(feed_steps):
        cols = pl.ds(k * width, width)
        value = dot_nn(r.normed_two[...], r.v_up[:, cols]) + r.up_bias[:, cols]
        r.active[:, cols] = gelu(value).astype(jnp.bfloat16)
        r.slope[:, cols] = value.astype(jnp.bfloat16)
    fed = dot_nn(r.active[...], r.v_down[...])
    r.out[...] = (fed + (r.residual[...] + r.down_bias[...])).astype(jnp.bfloat16)

    def pass_rows(src, dst, send, recv, section, first, turn):
        @pl.when(jnp.logical_not(first))
        def _():
            pl.semaphore_wait(turn, 1)

        remote(src, dst, send, recv, section, e).start()

        @pl.when(first)
        def _():
            sent(src, send)
            pl.semaphore_signal(
                turn, inc=1, device_id={"section": s, "dp": mate_core}, device_id_type=MESH
            )

    ahead = lax.rem(i, 2) == 0

    @pl.when(s < last)
    def _():
        @pl.when(i < group - 1)
        def _():
            remote(
                r.out.at[pl.ds(rows - HALO, HALO)],
                r.x.at[pl.ds(0, HALO)],
                r.pass_send_sem.at[1],
                r.pass_sem.at[1],
                s + 1,
                following,
            ).start()

        pass_rows(
            r.out,
            r.x.at[pl.ds(HALO, rows)],
            r.pass_send_sem.at[0],
            r.pass_sem.at[0],
            s + 1,
            ahead,
            r.turn.at[0],
        )

    def spread(stage, dst, send, recv):
        for section in range(sections):
            for h in range(2):
                start_to(
                    stage.at[h, pl.ds(section * share, share)],
                    dst.at[q],
                    send.at[section, h],
                    recv.at[q],
                    section,
                    2 * i + h,
                )

    def spread_sent(stage, send):
        for section in range(sections):
            for h in range(2):
                sent_to(
                    stage.at[h, pl.ds(section * share, share)],
                    send.at[section, h],
                    section,
                    2 * i + h,
                )

    def slope_step(step, carry):
        part = pl.ds(aligned(step * HALO, HALO), HALO)
        r.slope[part] = gelu_slope(r.slope[part].astype(jnp.float32)).astype(jnp.bfloat16)
        return carry

    lax.fori_loop(0, rows // HALO, slope_step, 0)

    z = e // 2
    line = parts // 2
    inner = (z > 0) & (z < line - 1)
    inwards = jnp.where(z == 0, e + 2, e - 2)

    def give(src, dst, index):
        return remote(
            src, dst, r.give_send_sem.at[index], r.give_sem.at[index], s, inwards
        )

    @pl.when((z == 0) | (z == line - 1))
    def _():
        give(r.normed_two, r.far_normed, 0).start()

    side = z // 2
    across = jnp.where(z < line // 2, e + 2, e - 2)
    unit = width // parts
    times = hidden_width // width
    tall = times * unit
    side_up, side_down = line * unit, line * tall

    def of_side(ref, which, count):
        return ref.at[:, pl.ds(aligned(which * count, LANES), count)]

    def cross(src, dst, kind, b):
        return remote(src, dst, r.cross_send_sem.at[kind, b], r.cross_sem.at[kind, b], s, across)

    def fetch(there, here, index):
        copy = pltpu.make_async_copy(there, here, r.far_load_sem.at[index])
        copy.start()
        return copy

    def each(count, body):
        def step(k, carry):
            body(k)
            return carry

        lax.fori_loop(0, count, step, 0)

    @pl.when(inner)
    def _():
        cross(r.normed_two, r.x_normed.at[0], 0, 0).start()
        arrived(r.far_normed, r.give_sem.at[0])
        cross(r.far_normed, r.x_normed.at[1], 0, 1).start()

    def work_out_others():
        copies = [fetch(r.far_normed, r.normed_side.at[0], 0)]
        for b in range(2):
            arrived(r.x_normed.at[b], r.cross_sem.at[0, b])
            copies.append(fetch(r.x_normed.at[b], r.normed_side.at[1 + b], 1 + b))
        for copy in copies:
            copy.wait()

        def other_step(step):
            b, k = step // times, lax.rem(step, times)
            cols = pl.ds(aligned(k * width, width), width)
            value = dot_nn(r.normed_side[b], r.v_up[:, cols]) + r.up_bias[:, cols]
            r.g_side[0] = gelu(value).astype(jnp.bfloat16)
            low = value.astype(jnp.bfloat16).astype(jnp.float32)
            r.g_side[1] = gelu_slope(low).astype(jnp.bfloat16)
            first = fetch(r.g_side.at[0], r.s_active.at[b, :, cols], 0)
            second = fetch(r.g_side.at[1], r.s_slope.at[b, :, cols], 1)
            first.wait()
            second.wait()

        each(3 * times, other_step)

    idle = s < last - 1

    @pl.when(inner & idle)
    def _():
        work_out_others()

    @pl.when(s < last)
    def _():
        other_chip(True)
        combine_far(True)
        arrived(r.g, r.grad_sem)


    @pl.when((z == 0) | (z == line - 1))
    def _():
        give(r.g, r.far_g, 1).start()

    @pl.when(inner)
    def _():
        cross(r.g, r.x_g.at[0], 1, 0).start()

    for k in range(feed_steps):
        cols = pl.ds(k * width, width)
        grad_active = dot_nt(r.g[...], r.v_down[cols, :])
        r.gh[:, cols] = (grad_active * r.slope[:, cols].astype(jnp.float32)).astype(jnp.bfloat16)
    r.acc[...] = dot_nt(r.gh[...], r.v_up[...])

    def norm_two_back(step, carry):
        gain_sum, bias_sum, out_sum = carry
        part = pl.ds(aligned(step * chunk, chunk), chunk)
        inverse = r.stats[part, 3:4]
        unit = (r.residual[part] - r.stats[part, 2:3]) * inverse
        grad = r.acc[part]
        value = r.g[part].astype(jnp.float32) + norm_backward(
            grad, unit, inverse, r.second_norm_gain[...]
        )
        r.g_res[part] = value
        low = value.astype(jnp.bfloat16)
        r.gb[part] = low
        return (
            gain_sum + col_sum(grad * unit),
            bias_sum + col_sum(grad),
            out_sum + col_sum(low.astype(jnp.float32)),
        )

    zero = jnp.zeros((1, width), jnp.float32)
    gain_sum, bias_sum, out_sum = lax.fori_loop(
        0, rows // chunk, norm_two_back, (zero, zero, zero)
    )
    r.v768[3:4] = out_sum
    r.v768[4:5] = gain_sum
    r.v768[5:6] = bias_sum
    r.acc[...] = dot_nt(r.gb[...], r.v_out[...])

    for k in range(pieces):
        cols = chunk_of(k)
        grad_conv = r.acc[:, cols] * r.short[:, cols]
        r.g_conv[:, cols] = grad_conv
        r.grad_send[k] = grad_conv.astype(jnp.bfloat16)
        send_piece(r.grad_send, k, True)
    transform(r.grad_send, r.wspec.at[order(True)])
    for k in range(pieces):
        cols = chunk_of(k)
        r.gs[pl.ds(0, rows), cols] = r.acc[:, cols] * r.conv_out[:, cols]
    @pl.when(s == last)
    def _():
        other_chip(True)
        combine_far(True)

    other_core(True)
    combine_near(True)
    found = inverse()
    for k in range(pieces):
        cols = chunk_of(k)
        gate_cols, value_cols = chunk_of(k, width), chunk_of(k, 2 * width)
        grad_middle = r.skip_gain[:, cols] * r.g_conv[:, cols] + found[:, k * wide : (k + 1) * wide]
        r.gs[pl.ds(0, rows), gate_cols] = grad_middle * r.short[:, value_cols]
        r.gs[pl.ds(0, rows), value_cols] = grad_middle * r.short[:, gate_cols]

    @pl.when(i > 0)
    def _():
        remote(
            r.gs.at[pl.ds(0, 8)],
            r.gs.at[pl.ds(rows, 8)],
            r.edge_send_sem,
            r.edge_sem,
            s,
            preceding,
        ).start()

    @pl.when(i == group - 1)
    def _():
        r.gs[pl.ds(rows, 8)] = jnp.zeros((8, 3 * width), jnp.float32)

    @pl.when(i < group - 1)
    def _():
        arrived(r.gs.at[pl.ds(rows, 8)], r.edge_sem)

    def mixed_back(cols):
        here = r.gs[pl.ds(0, rows), cols]
        w = r.short_weight
        value = w[0, :, cols] * here
        value = value + w[1, :, cols] * r.gs[pl.ds(1, rows), cols]
        value = value + w[2, :, cols] * r.gs[pl.ds(2, rows), cols]
        r.gm[:, cols] = value.astype(jnp.bfloat16)

    def in_back(k):
        cols = pl.ds(k * width, width)
        return dot_nt(r.gm[:, cols], r.v_in[:, cols])

    back = None
    for third in range(3):
        for k in range(pieces):
            mixed_back(chunk_of(k, third * width))
        if third > 0:
            back = in_back(third - 1) if back is None else back + in_back(third - 1)
    r.acc[...] = back + in_back(2)

    def norm_back(step, carry):
        gain_sum, bias_sum, down_sum = carry
        part = pl.ds(aligned(step * chunk, chunk), chunk)
        there = pl.ds(aligned(HALO + step * chunk, HALO), chunk)
        inverse = r.stats[there, 1:2]
        unit = (r.x[there].astype(jnp.float32) - r.stats[there, 0:1]) * inverse
        grad = r.acc[part]
        value = r.g_res[part] + norm_backward(grad, unit, inverse, r.norm_gain[...])
        r.g_res[part] = value
        r.g_pass[part] = value.astype(jnp.bfloat16)
        return (
            gain_sum + col_sum(grad * unit),
            bias_sum + col_sum(grad),
            down_sum + col_sum(r.g[part].astype(jnp.float32)),
        )

    gain_sum, bias_sum, down_sum = lax.fori_loop(0, rows // chunk, norm_back, (zero, zero, zero))
    r.v768[0:1] = gain_sum
    r.v768[1:2] = bias_sum
    r.v768[6:7] = down_sum
    r.v768[7:8] = zero

    @pl.when(s > 0)
    def _():
        pass_rows(
            r.g_pass,
            r.g,
            r.grad_send_sem,
            r.grad_sem,
            s - 1,
            jnp.logical_not(ahead),
            r.turn.at[1],
        )


    @pl.when(s == last)
    def _():
        length = r.lengths[q]
        for h in range(2):
            part = pl.ds(h * (rows // 2), rows // 2)
            place = lax.broadcasted_iota(jnp.int32, (rows // 2, 1), 0) + i * rows + h * (rows // 2)
            live = (place < length).astype(jnp.float32)
            r.stage[h] = turned(r.out[part].astype(jnp.float32) * live)
        spread(r.stage, r.outputs, r.show_send_sem, r.show_sem)

    @pl.when(s == 0)
    def _():
        for h in range(2):
            r.stage[h] = r.g_res[pl.ds(h * held, held)].T.astype(jnp.bfloat16)
        for section in range(sections):
            for h in range(2):
                src = r.stage.at[h, pl.ds(section * share, share)]
                if section == 0:
                    start_to(
                        src,
                        r.input_grad.at[q],
                        r.grad_show_send_sem.at[0, h],
                        r.grad_show_sem.at[q],
                        0,
                        2 * i + h,
                    )
                else:
                    remote(
                        src,
                        r.grad_relay.at[h],
                        r.grad_show_send_sem.at[section, h],
                        r.grad_relay_sem.at[h],
                        section,
                        e,
                    ).start()

    c = lax.rem(e, 2)
    half_rows = line * unit
    first_down, out_job, first_in, small_job = times, 2 * times, 2 * times + 1, 2 * times + 4

    def up_rows(k, start, count):
        cols = pl.ds(aligned(k * width, width), width)
        return r.v_up.at[pl.ds(aligned(start, HALO), count), cols]

    def down_rows(k, start, count):
        return r.v_down.at[pl.ds(aligned(k * width + start, HALO), count)]

    def out_rows(k, start, count):
        return r.v_out.at[pl.ds(aligned(start, HALO), count)]

    def in_rows(k, start, count):
        cols = pl.ds(aligned(k * width, width), width)
        return r.v_in.at[pl.ds(aligned(start, HALO), count), cols]

    def own_part(rows_of, k, owner):
        return rows_of(k, c * half_rows + owner * unit, unit)

    def to_mate(rows_of, k, j):
        src = rows_of(k, (1 - c) * half_rows, half_rows)
        remote(src, r.pair.at[j], r.pair_send_sem.at[j], r.pair_sem.at[j], s, mate_core).start()

    def add_to(ref, value):
        ref[...] = (ref[...].astype(jnp.float32) + value.astype(jnp.float32)).astype(ref.dtype)

    def merge_mate(rows_of, k, j):
        arrived(r.pair.at[j], r.pair_sem.at[j])
        copy = pltpu.make_async_copy(r.pair.at[j], r.pair_here, r.pair_load_sem)
        copy.start()
        copy.wait()
        for owner in range(line):
            add_to(own_part(rows_of, k, owner), r.pair_here[pl.ds(owner * unit, unit)])

    def send_line(src, dst, j, owner, slot, to):
        remote(src, dst, r.line_send_sem.at[j, owner], r.line_sem.at[j, slot], s, to).start()

    def line_slot(at, owner, rightward):
        return owner if rightward or owner < at else line

    def send_full(rows_of, k, j, lines, n, at, owner, add):
        rightward = owner > at
        src = own_part(rows_of, k, owner)
        if add:
            slot = line_slot(at, owner, rightward)
            arrived(lines.at[n, slot], r.line_sem.at[j, slot])
            add_to(src, lines[n, slot])
        after = at + (1 if rightward else -1)
        slot = line_slot(after, owner, rightward)
        send_line(src, lines.at[n, slot], j, owner, slot, e + 2 * (after - at))

    def start_full(rows_of, k, j, lines, n):
        for at in (0, line - 1):

            @pl.when(z == at)
            def _():
                for owner in sorted(range(line), key=lambda o: -abs(o - at)):
                    if owner != at:
                        send_full(rows_of, k, j, lines, n, at, owner, False)

    def pass_full(rows_of, k, j, lines, n, steps):
        for at in range(1, line - 1):

            @pl.when(z == at)
            def _():
                if at == steps:
                    for owner in range(line - 1, at, -1):
                        send_full(rows_of, k, j, lines, n, at, owner, True)
                if line - 1 - at == steps:
                    for owner in range(at):
                        send_full(rows_of, k, j, lines, n, at, owner, True)

    def store_partial(rows_of, k, value):
        for owner in range(parts):
            piece = value[owner * unit : (owner + 1) * unit]
            start = (owner % 2) * half_rows + (owner // 2) * unit
            rows_of(k, start, unit)[...] = piece.astype(jnp.bfloat16)

    kept = pl.ds(HALO, rows)

    store_partial(out_rows, 0, rows_product(r.gated[...], r.gb[...]))
    to_mate(out_rows, 0, out_job)

    def in_job(k):
        cols = pl.ds(aligned(k * width, width), width)
        store_partial(in_rows, k, rows_product(r.normed[kept], r.gm[:, cols]))
        to_mate(in_rows, k, first_in + k)

    each(3, in_job)
    merge_mate(out_rows, 0, out_job)
    start_full(out_rows, 0, out_job, r.full_line, 0)

    def merge_in(k):
        merge_mate(in_rows, k, first_in + k)
        start_full(in_rows, k, first_in + k, r.full_line, 1 + k)

    each(3, merge_in)

    def sums_step(b, carry):
        cols = lanes_of(b)
        here = r.gs[pl.ds(0, rows), cols]
        r.v2304[0:1, cols] = col_sum(r.gm[:, cols].astype(jnp.float32))
        for tap in range(3):
            r.v2304[1 + tap : 2 + tap, cols] = col_sum(
                here * r.mixed[pl.ds(HALO - tap, rows), cols]
            )
        r.v2304[4:5, cols] = col_sum(here)
        return carry

    lax.fori_loop(0, 3 * blocks, sums_step, 0)
    r.v2304[5:8] = jnp.zeros((3, 3 * width), jnp.float32)
    for k in range(pieces):
        cols = chunk_of(k)
        middle = r.short[:, chunk_of(k, width)] * r.short[:, chunk_of(k, 2 * width)]
        r.v768[2:3, cols] = col_sum(r.g_conv[:, cols] * middle)
    for step in range(hidden_width // width):
        cols = pl.ds(step * width, width)
        r.v3072[:, cols] = col_sum(r.gh[:, cols].astype(jnp.float32))
    mine = order(True)

    def filter_rows(step, carry):
        m = step // (pieces * (rows // fine_rows))
        k = lax.rem(step // (rows // fine_rows), pieces)
        start = aligned(lax.rem(step, rows // fine_rows) * fine_rows, fine_rows)
        upper, lower = pl.ds(start, fine_rows), pl.ds(rows + start, fine_rows)
        a = r.wspec[mine, k, upper].astype(jnp.float32)
        b = r.wspec[mine, k, lower].astype(jnp.float32)
        turn = 1.0 - 2.0 * lax.rem(
            lax.broadcasted_iota(jnp.int32, (fine_rows, 1), 0), jnp.int32(2)
        ).astype(jnp.float32)
        turn = jnp.where(m < i, turn, 0.0)

        def against(j):
            u = r.zspec[j, k, upper].astype(jnp.float32)
            v = r.zspec[j, k, lower].astype(jnp.float32)
            return (a * u + b * v, b * u - a * v)

        even, odd = against(i - m)
        next_even, next_odd = against(jnp.maximum(i - m - 1, 0))
        r.zspec[i - m, k, upper] = (even - turn * next_odd).astype(jnp.bfloat16)
        r.zspec[i - m, k, lower] = (odd + turn * next_even).astype(jnp.bfloat16)
        return carry

    lax.fori_loop(0, (i + 1) * pieces * (rows // fine_rows), filter_rows, 0)
    quarter = half_rows // 2

    def side_part(rows_of, k, h):
        return rows_of(k, c * quarter + h * unit, unit)

    def side_to_mate(rows_of, k, j):
        src = rows_of(k, (1 - c) * quarter, quarter)
        return remote(
            src,
            r.pair.at[j, pl.ds(0, quarter)],
            r.pair_send_sem.at[j],
            r.pair_sem.at[j],
            s,
            mate_core,
        )

    def side_edge(rows_of, k, j):
        edge = jnp.where(side == 0, 0, line - 1)
        to = jnp.where(side == 0, e - 2, e + 2)
        return remote(
            side_part(rows_of, k, side),
            r.inner_line.at[j],
            r.line_send_sem.at[j, edge],
            r.line_sem.at[j, 0],
            s,
            to,
        )

    def side_merge(rows_of, k, j):
        here = pl.ds(0, quarter)
        arrived(r.pair.at[j, here], r.pair_sem.at[j])
        copy = pltpu.make_async_copy(r.pair.at[j, here], r.pair_here.at[here], r.pair_load_sem)
        copy.start()
        copy.wait()
        for h in range(2):
            add_to(side_part(rows_of, k, h), r.pair_here[pl.ds(h * unit, unit)])
        side_edge(rows_of, k, j).start()

    def side_store(rows_of, k, share_index, piece):
        start = lax.rem(share_index, 2) * quarter + (share_index // 2) * unit
        rows_of(k, start, unit)[...] = piece.astype(jnp.bfloat16)

    @pl.when(inner & jnp.logical_not(idle))
    def _():
        work_out_others()

    @pl.when(inner)
    def _():
        arrived(r.far_g, r.give_sem.at[1])
        cross(r.far_g, r.x_g.at[1], 1, 1).start()
        copies = [fetch(r.far_g, r.x.at[kept], 0)]
        for b in range(2):
            arrived(r.x_g.at[b], r.cross_sem.at[1, b])
            copies.append(fetch(r.x_g.at[b], r.g_side.at[b], 1 + b))
        for copy in copies:
            copy.wait()

        def staged(b):
            return r.slope.at[:, pl.ds(b * width, width)]

        def up_side(k):
            cols = pl.ds(aligned(k * width, width), width)
            loads = [fetch(r.s_slope.at[b, :, cols], staged(b), b) for b in range(3)]
            own = of_side(r.normed_two, side, side_up)
            value = rows_product(own[...], r.gh[:, cols])
            for b, grads in enumerate((r.x.at[kept], r.g_side.at[0], r.g_side.at[1])):
                grad = dot_nt(grads[...], r.v_down[cols, :])
                loads[b].wait()
                grad = (grad * staged(b)[...].astype(jnp.float32)).astype(jnp.bfloat16)
                value = value + rows_product(of_side(r.normed_side.at[b], side, side_up)[...], grad)
            for n in range(line):
                side_store(up_rows, k, n, value[n * unit : (n + 1) * unit])
            side_to_mate(up_rows, k, k).start()

            @pl.when(k > 0)
            def _():
                side_merge(up_rows, k - 1, k - 1)

        each(times, up_side)
        pass_full(out_rows, 0, out_job, r.full_line, 0, 1)
        homes = (r.slope.at[:, :side_down], r.slope.at[:, side_down:], r.gh.at[:, :side_down])
        copies = [
            fetch(of_side(r.s_active.at[b], side, side_down), homes[b], b) for b in range(3)
        ]
        side_merge(up_rows, times - 1, times - 1)
        for copy in copies:
            copy.wait()

        def down_side(n):
            cols = pl.ds(aligned(n * tall, tall), tall)
            second = pl.ds(aligned(side_down + n * tall, tall), tall)
            mine = pl.ds(aligned(side * side_down + n * tall, tall), tall)
            value = rows_product(r.active[:, mine], r.g[...])
            value = value + rows_product(r.slope[:, cols], r.x[kept])
            value = value + rows_product(r.slope[:, second], r.g_side[0])
            value = value + rows_product(r.gh[:, cols], r.g_side[1])
            for k in range(times):
                side_store(down_rows, k, n, value[unit * k : unit * (k + 1)])

        each(line, down_side)
        each(times, lambda k: side_to_mate(down_rows, k, first_down + k).start())
        pass_full(in_rows, 0, first_in, r.full_line, 1, 1)
        each(times, lambda k: side_merge(down_rows, k, first_down + k))

    filt = r.filter_two.shape[0]

    def filter_back(step, carry):
        g_one, g_one_bias, g_two, g_two_bias, g_out, g_out_bias = carry
        part = pl.ds(aligned(step * rows, rows), rows)
        layer_one, layer_two, one, two = filter_layers(r, part)
        low_two = layer_two.astype(jnp.bfloat16)
        back = jnp.zeros((rows, filt), jnp.float32)
        out_parts, bias_parts = [], []
        for k in range(pieces):
            cols = pl.ds(k * wide, wide)
            grad = dot_nn(r.waves_back[...], r.zspec[i - step, k]) * (1.0 / rows)
            grad = grad * jnp.exp(-r.decay[:, cols] * scaled_place(step))
            low = grad.astype(jnp.bfloat16)
            back = back + dot_nt(low, r.filter_out[:, cols].astype(jnp.bfloat16))
            out_parts.append(rows_product(low_two, low))
            bias_parts.append(col_sum(grad))
        back = back * (sine_scale * jnp.cos(two))
        low = back.astype(jnp.bfloat16)
        front = dot_nt(low, r.filter_two[...].astype(jnp.bfloat16)) * (sine_scale * jnp.cos(one))
        high = r.features[part, :FEATURE_ROWS]
        return (
            g_one + rows_product(front.astype(jnp.bfloat16), high),
            g_one_bias + col_sum(front),
            g_two + rows_product(layer_one.astype(jnp.bfloat16), low),
            g_two_bias + col_sum(back),
            g_out + jnp.concatenate(out_parts, axis=1),
            g_out_bias + jnp.concatenate(bias_parts, axis=1),
        )

    shapes = (
        (filt, FEATURE_ROWS),
        (1, filt),
        (filt, filt),
        (1, filt),
        (filt, width),
        (1, width),
    )
    zeros = tuple(jnp.zeros(shape, jnp.float32) for shape in shapes)
    g_one, g_one_bias, g_two, g_two_bias, g_out, g_out_bias = lax.fori_loop(
        0, i + 1, filter_back, zeros
    )
    r.small[...] = jnp.zeros(r.small.shape, jnp.float32)
    few = filt // parts
    for owner in range(parts):
        y, x = owner % 2, owner // 2
        r.small[y, x, 0:8, :unit] = r.v768[:, unit * owner : unit * (owner + 1)]
        r.small[y, x, 7:8, :unit] = g_out_bias[:, unit * owner : unit * (owner + 1)]
        for m in range(3):
            start = 3 * unit * owner + unit * m
            r.small[y, x, 8 * (m + 1) : 8 * (m + 2), :unit] = r.v2304[:, start : start + unit]
            start = 3 * LANES * owner + LANES * m
            r.small[y, x, 8 * m + 13 : 8 * m + 14] = r.v3072[:, start : start + LANES]
        mine = slice(few * owner, few * (owner + 1))
        r.small[y, x, 14:15, :few] = g_one_bias[:, mine]
        r.small[y, x, 15:16, :few] = g_two_bias[:, mine]
        r.small[y, x, 32 : 32 + few, : g_one.shape[1]] = g_one[mine]
        r.small[y, x, 40 : 40 + few, :filt] = g_two[mine]
        for b in range(blocks):
            row = 48 + 8 * b
            r.small[y, x, row : row + few] = g_out[mine, b * LANES : (b + 1) * LANES]


    def small_rows(k, start, count):
        return r.small.at[start // half_rows, lax.rem(start, half_rows) // unit]

    remote(
        r.small.at[1 - c],
        r.small_pair,
        r.pair_send_sem.at[small_job],
        r.pair_sem.at[small_job],
        s,
        mate_core,
    ).start()
    arrived(r.small_pair, r.pair_sem.at[small_job])
    r.small[c] += r.small_pair[...]
    start_full(small_rows, 0, small_job, r.small_line, 0)

    def arrive_full(j, lines, n, into):
        for at in range(line):
            slots = ([at] if at > 0 else []) + ([line] if at < line - 1 else [])

            @pl.when(z == at)
            def _():
                for slot in slots:
                    arrived(lines.at[n, slot], r.line_sem.at[j, slot])
                    into[...] += lines[n, slot].astype(jnp.float32)

    depth = r.ready.shape[0]

    def to_result(j, there):
        slot = lax.rem(j, depth)
        return pltpu.make_async_copy(r.ready.at[slot], there, r.result_sem.at[slot])

    def free_result(j):
        @pl.when(j >= depth)
        def _():
            to_result(j, r.out_grad).wait()

    def finish_inner(rows_of, k, j, there):
        free_result(j)
        into = r.ready.at[lax.rem(j, depth)]

        @pl.when(inner)
        def _():
            into[...] = side_part(rows_of, k, 1 - side)[...].astype(jnp.float32)

        @pl.when(jnp.logical_not(inner))
        def _():
            arrived(r.inner_line.at[j], r.line_sem.at[j, 0])
            into[...] = r.inner_line[j].astype(jnp.float32)

        to_result(j, there).start()

    def finish_full(rows_of, k, j, n, there):
        free_result(j)
        into = r.ready.at[lax.rem(j, depth)]
        into[...] = own_part(rows_of, k, z)[...].astype(jnp.float32)
        arrive_full(j, r.full_line, n, into)
        to_result(j, there).start()

    def wide_place(ref, k):
        return ref.at[:, pl.ds(aligned(k * width, width), width)]

    def tall_place(ref, k):
        return ref.at[pl.ds(aligned(k * unit, HALO), unit)]

    each(times, lambda k: finish_inner(up_rows, k, k, wide_place(r.up_grad, k)))

    @pl.when(inner)
    def _():
        each(2, lambda k: pass_full(in_rows, 1 + k, first_in + 1 + k, r.full_line, 2 + k, 1))
        pass_full(small_rows, 0, small_job, r.small_line, 0, 1)

        for steps in range(2, line - 1):
            pass_full(out_rows, 0, out_job, r.full_line, 0, steps)
            each(3, lambda k: pass_full(in_rows, k, first_in + k, r.full_line, 1 + k, steps))
            pass_full(small_rows, 0, small_job, r.small_line, 0, steps)

    each(
        times, lambda k: finish_inner(down_rows, k, first_down + k, tall_place(r.down_grad, k))
    )
    finish_full(out_rows, 0, out_job, 0, r.out_grad)
    each(3, lambda k: finish_full(in_rows, k, first_in + k, 1 + k, wide_place(r.in_grad, k)))
    for j in range(small_job - depth, small_job):
        to_result(j, r.out_grad).wait()
    r.small_sum[...] = r.small[c, z]
    arrive_full(small_job, r.small_line, 0, r.small_sum)
    got = r.small_sum
    for row, out in enumerate(
        (
            r.norm_gain_grad,
            r.norm_bias_grad,
            r.skip_gain_grad,
            r.out_bias_grad,
            r.second_gain_grad,
            r.second_bias_grad,
            r.down_bias_grad,
            r.filter_out_bias_grad,
        )
    ):
        out[...] = got[row : row + 1, :unit]
    for m in range(3):
        lanes = slice(unit * m, unit * (m + 1))
        r.in_bias_grad[:, lanes] = got[8 * (m + 1) : 8 * (m + 1) + 1, :unit]
        for tap in range(3):
            row = 8 * (m + 1) + 1 + tap
            r.short_weight_grad[tap, :, lanes] = got[row : row + 1, :unit]
        r.short_bias_grad[:, lanes] = got[8 * (m + 1) + 4 : 8 * (m + 1) + 5, :unit]
        r.up_bias_grad[:, LANES * m : LANES * (m + 1)] = got[8 * m + 13 : 8 * m + 14]
    r.filter_one_bias_grad[...] = got[14:15, :few]
    r.filter_two_bias_grad[...] = got[15:16, :few]
    r.filter_one_grad[...] = got[32 : 32 + few, : r.filter_one_grad.shape[1]]
    r.filter_two_grad[...] = got[40 : 40 + few, :filt]
    for b in range(blocks):
        r.filter_out_grad[:, b * LANES : (b + 1) * LANES] = got[48 + 8 * b : 48 + 8 * b + few]

    def line_sent(j, owner, src):
        sent(src, r.line_send_sem.at[j, owner])

    def sends_end(rows_of, k, j):
        for owner in range(line):

            @pl.when(z != owner)
            def _():
                line_sent(j, owner, own_part(rows_of, k, owner))

    def mate_sent(rows_of, k, j):
        sent(rows_of(k, (1 - c) * half_rows, half_rows), r.pair_send_sem.at[j])

    @pl.when(inner)
    def _():
        cross(r.normed_two, r.x_normed.at[0], 0, 0).wait_send()
        cross(r.far_normed, r.x_normed.at[1], 0, 1).wait_send()
        cross(r.g, r.x_g.at[0], 1, 0).wait_send()
        cross(r.far_g, r.x_g.at[1], 1, 1).wait_send()
        for rows_of, first in ((up_rows, 0), (down_rows, first_down)):

            def end_side(k):
                side_to_mate(rows_of, k, first + k).wait_send()
                side_edge(rows_of, k, first + k).wait_send()

            each(times, end_side)

    mate_sent(out_rows, 0, out_job)
    sends_end(out_rows, 0, out_job)

    def end_in(k):
        mate_sent(in_rows, k, first_in + k)
        sends_end(in_rows, k, first_in + k)

    each(3, end_in)
    sent(r.small.at[1 - c], r.pair_send_sem.at[small_job])
    sends_end(small_rows, 0, small_job)

    @pl.when(s == 0)
    def _():
        for section in range(sections):
            for h in range(2):
                src = r.stage.at[h, pl.ds(section * share, share)]
                if section == 0:
                    sent_to(src, r.grad_show_send_sem.at[0, h], 0, 2 * i + h)
                else:
                    sent(src, r.grad_show_send_sem.at[section, h])

    @pl.when(s > 0)
    def _():
        for h in range(2):
            arrived(r.grad_relay.at[h], r.grad_relay_sem.at[h])
            start_to(
                r.grad_relay.at[h],
                r.input_grad.at[q],
                r.grad_hand_sem.at[h],
                r.grad_show_sem.at[q],
                s,
                2 * i + h,
            )
        for h in range(2):
            sent_to(r.grad_relay.at[h], r.grad_hand_sem.at[h], s, 2 * i + h)

    for m in range(micro):
        arrived(r.input_grad.at[m], r.grad_show_sem.at[m])

    for m in range(micro):
        dp = holder(m, pos)
        sent_to(r.inputs.at[m], r.in_send_sem.at[m], 0, dp)
        sent_to(r.cot.at[m], r.cot_send_sem.at[m], last, dp)

        @pl.when(halo_there)
        def _():
            sent_to(r.inputs.at[m], r.halo_send_sem.at[m], 0, holder(m, pos + 1))

    @pl.when(jnp.logical_not(inner))
    def _():
        give(r.normed_two, r.far_normed, 0).wait_send()
        give(r.g, r.far_g, 1).wait_send()

    pieces_sent(r.mid_send, False)
    pieces_sent(r.grad_send, True)

    @pl.when(i > 0)
    def _():
        sent(r.gs.at[pl.ds(0, 8)], r.edge_send_sem)

    @pl.when(s < last)
    def _():
        @pl.when(jnp.logical_not(ahead))
        def _():
            sent(r.out, r.pass_send_sem.at[0])

        @pl.when(i < group - 1)
        def _():
            sent(r.out.at[pl.ds(rows - HALO, HALO)], r.pass_send_sem.at[1])

    @pl.when(s == last)
    def _():
        spread_sent(r.stage, r.show_send_sem)

    @pl.when((s > 0) & ahead)
    def _():
        sent(r.g_pass, r.grad_send_sem)

    for m in range(micro):
        arrived(r.outputs.at[m], r.show_sem.at[m])


def chain_call(geometry, operands):
    sections, parts, group, rows, width, hidden_width = geometry
    total = group * rows
    blocks = width // LANES
    share = width // sections
    wide = 2 * LANES
    pieces = width // wide
    micro, _, held = operands["inputs"].shape
    unit = width // parts
    line = parts // 2
    times = hidden_width // width
    filt = operands["filter_two"].shape[0]
    few = filt // parts
    f32, bf16 = jnp.float32, jnp.bfloat16
    anywhere = pl.BlockSpec(memory_space=pl.ANY)
    vmem = pl.BlockSpec(memory_space=pltpu.VMEM)
    smem = pl.BlockSpec(memory_space=pltpu.SMEM)
    in_specs = [anywhere] * FAR + [smem] + [vmem] * (len(operands) - FAR - 1)
    outs = dict(
        outputs=((micro, share, held), bf16, anywhere),
        input_grad=((micro, share, held), bf16, anywhere),
        norm_gain_grad=((1, unit), f32, vmem),
        norm_bias_grad=((1, unit), f32, vmem),
        in_grad=((unit, 3 * width), f32, anywhere),
        in_bias_grad=((1, 3 * unit), f32, vmem),
        short_weight_grad=((3, 1, 3 * unit), f32, vmem),
        short_bias_grad=((1, 3 * unit), f32, vmem),
        filter_one_grad=((few, EMB), f32, vmem),
        filter_one_bias_grad=((1, few), f32, vmem),
        filter_two_grad=((few, filt), f32, vmem),
        filter_two_bias_grad=((1, few), f32, vmem),
        filter_out_grad=((few, width), f32, vmem),
        filter_out_bias_grad=((1, unit), f32, vmem),
        skip_gain_grad=((1, unit), f32, vmem),
        out_grad=((unit, width), f32, anywhere),
        out_bias_grad=((1, unit), f32, vmem),
        second_gain_grad=((1, unit), f32, vmem),
        second_bias_grad=((1, unit), f32, vmem),
        up_grad=((unit, hidden_width), f32, anywhere),
        up_bias_grad=((1, times * unit), f32, vmem),
        down_grad=((times * unit, width), f32, anywhere),
        down_bias_grad=((1, unit), f32, vmem),
        far_normed=((rows, width), bf16, anywhere),
        far_g=((rows, width), bf16, anywhere),
        pair=((2 * times + 4, line * unit, width), bf16, anywhere),
        x_normed=((2, rows, width), bf16, anywhere),
        x_g=((2, rows, width), bf16, anywhere),
        s_active=((3, rows, hidden_width), bf16, anywhere),
        s_slope=((3, rows, hidden_width), bf16, anywhere),
        grad_relay=((2, share, held), bf16, anywhere),
    )
    dma = pltpu.SemaphoreType.DMA
    scratch = dict(
        v_in=pltpu.VMEM((width, 3 * width), bf16),
        v_out=pltpu.VMEM((width, width), bf16),
        v_up=pltpu.VMEM((width, hidden_width), bf16),
        v_down=pltpu.VMEM((hidden_width, width), bf16),
        x=pltpu.VMEM((HALO + rows, width), bf16),
        normed=pltpu.VMEM((HALO + rows, width), bf16),
        mixed=pltpu.VMEM((HALO + rows, 3 * width), f32),
        short=pltpu.VMEM((rows, 3 * width), f32),
        mid_send=pltpu.VMEM((pieces, rows, wide), bf16),
        grad_send=pltpu.VMEM((pieces, rows, wide), bf16),
        far=pltpu.VMEM((group - 1, pieces, rows, wide), bf16),
        far_back=pltpu.VMEM((group - 1, pieces, rows, wide), bf16),
        kspec=pltpu.VMEM((group, pieces, 2 * rows, wide), bf16),
        zspec=pltpu.VMEM((group, pieces, 2 * rows, wide), bf16),
        wspec=pltpu.VMEM((group, pieces, 2 * rows, wide), bf16),
        yspec=pltpu.VMEM((pieces, 2 * rows, wide), bf16),
        conv_out=pltpu.VMEM((rows, width), f32),
        gated=pltpu.VMEM((rows, width), bf16),
        residual=pltpu.VMEM((rows, width), f32),
        normed_two=pltpu.VMEM((rows, width), bf16),
        slope=pltpu.VMEM((rows, hidden_width), bf16),
        active=pltpu.VMEM((rows, hidden_width), bf16),
        acc=pltpu.VMEM((rows, width), f32),
        out=pltpu.VMEM((rows, width), bf16),
        g=pltpu.VMEM((rows, width), bf16),
        gh=pltpu.VMEM((rows, hidden_width), bf16),
        g_res=pltpu.VMEM((rows, width), f32),
        gb=pltpu.VMEM((rows, width), bf16),
        g_conv=pltpu.VMEM((rows, width), f32),
        gs=pltpu.VMEM((rows + 8, 3 * width), f32),
        gm=pltpu.VMEM((rows, 3 * width), bf16),
        g_pass=pltpu.VMEM((rows, width), bf16),
        in_recv=pltpu.VMEM((2, width, held), bf16),
        in_halo=pltpu.VMEM((width, held), bf16),
        cot_recv=pltpu.VMEM((2, width, held), bf16),
        stage=pltpu.VMEM((2, width, held), bf16),
        load_sem=dma((4,)),
        v768=pltpu.VMEM((8, width), f32),
        v2304=pltpu.VMEM((8, 3 * width), f32),
        v3072=pltpu.VMEM((1, hidden_width), f32),
        normed_side=pltpu.VMEM((3, rows, width), bf16),
        g_side=pltpu.VMEM((2, rows, width), bf16),
        pair_here=pltpu.VMEM((line * unit, width), bf16),
        inner_line=pltpu.VMEM((2 * times, unit, width), bf16),
        full_line=pltpu.VMEM((4, line + 1, unit, width), bf16),
        small=pltpu.VMEM((2, line, SMALL, LANES), f32),
        small_pair=pltpu.VMEM((line, SMALL, LANES), f32),
        small_line=pltpu.VMEM((1, line + 1, SMALL, LANES), f32),
        small_sum=pltpu.VMEM((SMALL, LANES), f32),
        ready=pltpu.VMEM((3, unit, width), f32),
        stats=pltpu.VMEM((HALO + rows, 4), f32),
        pair_send_sem=dma((2 * times + 5,)),
        pair_sem=dma((2 * times + 5,)),
        pair_load_sem=dma,
        line_send_sem=dma((2 * times + 5, line)),
        line_sem=dma((2 * times + 5, line + 1)),
        far_load_sem=dma((6,)),
        cross_send_sem=dma((2, 2)),
        cross_sem=dma((2, 2)),
        result_sem=dma((3,)),
        grad_show_send_sem=dma((sections, 2)),
        grad_show_sem=dma((micro,)),
        grad_relay_sem=dma((2,)),
        grad_hand_sem=dma((2,)),
        in_send_sem=dma((micro,)),
        in_sem=dma((sections, 2)),
        halo_send_sem=dma((micro,)),
        halo_sem=dma((sections,)),
        cot_send_sem=dma((micro,)),
        cot_sem=dma((sections, 2)),
        near_send_sem=dma((2, pieces)),
        near_back_send_sem=dma((2, pieces)),
        hand_send_sem=dma((pieces,)),
        hand_back_send_sem=dma((pieces,)),
        far_sem=dma((group - 1, pieces)),
        far_back_sem=dma((group - 1, pieces)),
        give_send_sem=dma((2,)),
        give_sem=dma((2,)),
        pass_send_sem=dma((2,)),
        pass_sem=dma((2,)),
        turn=pltpu.SemaphoreType.REGULAR((2,)),
        grad_send_sem=dma,
        grad_sem=dma,
        edge_send_sem=dma,
        edge_sem=dma,
        show_send_sem=dma((sections, 2)),
        show_sem=dma((micro,)),
    )
    names = tuple(operands) + tuple(outs) + tuple(scratch)
    results = pl.pallas_call(
        functools.partial(chain_kernel, geometry, names),
        out_shape=[jax.ShapeDtypeStruct(shape, dtype) for shape, dtype, _ in outs.values()],
        in_specs=in_specs,
        out_specs=[spec for _, _, spec in outs.values()],
        scratch_shapes=list(scratch.values()),
        compiler_params=pltpu.CompilerParams(
            collective_id=0, has_side_effects=True, vmem_limit_bytes=62 * 1024 * 1024
        ),
        name="chain",
    )(*operands.values())
    return types.SimpleNamespace(**dict(zip(outs, results)))


def store_kernel(count, widened, *refs):
    source, result, held, sem = refs[:count], refs[count : 2 * count], refs[2 * count : -2], refs[-1]
    wide = refs[-2]
    loads = [pltpu.make_async_copy(source[k], held[k], sem.at[0, k]) for k in range(count)]
    stores = [
        pltpu.make_async_copy(wide if k == widened else held[k], result[k], sem.at[1, k])
        for k in range(count)
    ]
    for copy in loads:
        copy.start()
    for k in range(count):
        loads[k].wait()
        if k == widened:
            wide[...] = held[k][...].astype(jnp.float32)
        stores[k].start()
    for copy in stores:
        copy.wait()


def store_call(arrays, widened=1):
    anywhere = pl.BlockSpec(memory_space=pl.ANY)
    count = len(arrays)
    types_out = [jnp.float32 if k == widened else array.dtype for k, array in enumerate(arrays)]
    return pl.pallas_call(
        functools.partial(store_kernel, count, widened),
        out_shape=[
            jax.ShapeDtypeStruct(array.shape, dtype) for array, dtype in zip(arrays, types_out)
        ],
        in_specs=[anywhere] * count,
        out_specs=[anywhere] * count,
        scratch_shapes=[pltpu.VMEM(array.shape, array.dtype) for array in arrays]
        + [pltpu.VMEM(arrays[widened].shape, jnp.float32), pltpu.SemaphoreType.DMA((2, count))],
        compiler_params=pltpu.CompilerParams(vmem_limit_bytes=62 * 1024 * 1024),
        name="store",
    )(*arrays)


def wave_matrices(rows):
    angles = np.pi * ((2 * np.arange(rows)[:, None] + 1) * np.arange(rows)[None, :] % (4 * rows))
    angles = angles / (2.0 * rows)
    waves = np.concatenate([np.cos(angles), np.sin(angles)], axis=0).astype(jnp.bfloat16)
    return (jnp.asarray(waves), jnp.asarray(np.ascontiguousarray(waves.T)))


def feature_table(total):
    places = np.arange(total)
    frequency = np.arange(1, (EMB - 1) // 2 + 1)
    angles = 2.0 * np.pi * (places[:, None] * frequency[None, :] % total) / total
    scaled = places[:, None] / total
    table = np.concatenate([scaled, np.cos(angles), np.sin(angles)], axis=1).astype(np.float32)
    table = np.pad(table, ((0, 0), (0, FEATURE_ROWS - EMB)))
    high = table.astype(jnp.bfloat16)
    low = (table - high.astype(np.float32)).astype(jnp.bfloat16)
    table = np.concatenate([high, low, high], axis=1)
    return jnp.asarray(table)


def local_line(sections, parts, *args):
    (
        inputs,
        cotangent,
        seq_lengths,
        decay_rates,
        norm_gain,
        norm_bias,
        in_weight,
        in_bias,
        short_weight,
        short_bias,
        filter_weight_one,
        filter_bias_one,
        filter_weight_two,
        filter_bias_two,
        filter_weight_out,
        filter_bias_out,
        skip_gain,
        out_weight,
        out_bias,
        second_norm_gain,
        second_norm_bias,
        up_weight,
        up_bias,
        down_weight,
        down_bias,
    ) = args
    micro, held, share = inputs.shape
    width, hidden_width = up_weight.shape[1:]
    group = parts // micro
    total = parts * held
    rows = total // group
    geometry = (sections, parts, group, rows, width, hidden_width)
    features = feature_table(total)
    waves, waves_back = wave_matrices(rows)
    operands = dict(
        inputs=jnp.swapaxes(inputs, 1, 2),
        cot=jnp.swapaxes(cotangent, 1, 2),
        w_in=in_weight[0],
        w_out=out_weight[0],
        w_up=up_weight[0],
        w_down=down_weight[0],
        lengths=seq_lengths,
        features=features,
        waves_back=waves_back,
        decay=decay_rates,
        filter_one=jnp.swapaxes(filter_weight_one, 0, 1),
        filter_one_bias=filter_bias_one,
        filter_two=filter_weight_two[0],
        filter_two_bias=filter_bias_two,
        filter_out=filter_weight_out[0],
        filter_out_bias=filter_bias_out,
        waves=waves,
        norm_gain=norm_gain,
        norm_bias=norm_bias,
        in_bias=in_bias,
        short_weight=jnp.swapaxes(short_weight, 0, 1),
        short_bias=short_bias,
        skip_gain=skip_gain,
        out_bias=out_bias,
        second_norm_gain=second_norm_gain,
        second_norm_bias=second_norm_bias,
        up_bias=up_bias,
        down_bias=down_bias,
    )
    made = chain_call(geometry, operands)
    names = list(vars(made))[:-8]
    stored = store_call([getattr(made, name) for name in names])
    sums = types.SimpleNamespace(**dict(zip(names, stored)))
    return (
        jnp.swapaxes(sums.outputs, 1, 2),
        jnp.swapaxes(sums.input_grad, 1, 2),
        sums.norm_gain_grad,
        sums.norm_bias_grad,
        sums.in_grad[None],
        sums.in_bias_grad,
        jnp.swapaxes(sums.short_weight_grad, 0, 1),
        sums.short_bias_grad,
        sums.filter_one_grad.T[None],
        sums.filter_one_bias_grad,
        sums.filter_two_grad[None],
        sums.filter_two_bias_grad,
        sums.filter_out_grad[None],
        sums.filter_out_bias_grad,
        sums.skip_gain_grad,
        sums.out_grad[None],
        sums.out_bias_grad,
        sums.second_gain_grad,
        sums.second_bias_grad,
        sums.up_grad[None],
        sums.up_bias_grad,
        sums.down_grad[None],
        sums.down_bias_grad,
    )


def fits_line(mesh, inputs, up_weight):
    sections, parts = mesh.shape["section"], mesh.shape["dp"]
    micro, tokens, width = inputs.shape
    return (
        parts == 4 * micro
        and tokens == 1024
        and width == 6 * LANES
        and up_weight.shape[2] == 4 * width
        and width % sections == 0
        and sections > 1
    )


def solution(mesh):
    in_specs = (
        P(None, "dp", "section"),
        P(None, "dp", "section"),
        P(),
        P("section", None),
        P("section", None),
        P("section", None),
        P("section", None, None),
        P("section", None),
        P("section", None, None),
        P("section", None),
        P("section", None, None),
        P("section", None),
        P("section", None, None),
        P("section", None),
        P("section", None, None),
        P("section", None),
        P("section", None),
        P("section", None, None),
        P("section", None),
        P("section", None),
        P("section", None),
        P("section", None, None),
        P("section", None),
        P("section", None, None),
        P("section", None),
    )
    out_specs = (
        P(None, "dp", "section"),
        P(None, "dp", "section"),
        P("section", "dp"),
        P("section", "dp"),
        P("section", "dp", None),
        P("section", "dp"),
        P("section", None, "dp"),
        P("section", "dp"),
        P("section", None, "dp"),
        P("section", "dp"),
        P("section", "dp", None),
        P("section", "dp"),
        P("section", "dp", None),
        P("section", "dp"),
        P("section", "dp"),
        P("section", "dp", None),
        P("section", "dp"),
        P("section", "dp"),
        P("section", "dp"),
        P("section", "dp", None),
        P("section", "dp"),
        P("section", "dp", None),
        P("section", "dp"),
    )

    def whole(*args):
        if fits_line(mesh, args[0], args[21]):
            body = functools.partial(local_line, mesh.shape["section"], mesh.shape["dp"])
        else:
            body = local_general
        return jax.shard_map(
            body, mesh=mesh, in_specs=in_specs, out_specs=out_specs, check_vma=False
        )(*args)

    return whole
```
